256 devices in a mesh: ep: 64 (over y, z, core), dp: 4 (over x).
Axes of the slice: x: 4, y: 4, z: 8, core: 2. Of those that a mesh axis runs over, the one named last changes fastest.
Arguments:
- tokens: bfloat16 [32768, 2048], P(('dp', 'ep')), parts along dimension 0, may hold values from -6 to 6
- routes: int32 [32768, 10], P(('dp', 'ep')), parts along dimension 0, may hold values from 0 to 63, all different within a row; in each aligned block of 128 rows (0 to 127, 128 to 255, ...) at most 24 rows name the same one
- gate_share: float32 [32768, 10], P(('dp', 'ep')), parts along dimension 0, may hold values from 0.1 to 1
- norm_gain: float32 [2048], replicated, may hold values from 0.1 to 1.9
- w_gate: bfloat16 [64, 2048, 512], P('ep'), may hold values from -0.125 to 0.125
- w_up: bfloat16 [64, 2048, 512], P('ep'), may hold values from -0.125 to 0.125
- w_down: bfloat16 [64, 512, 2048], P('ep'), may hold values from -0.25 to 0.25
- shared_gate: bfloat16 [2048, 256], replicated, may hold values from -0.125 to 0.125
- shared_up: bfloat16 [2048, 256], replicated, may hold values from -0.125 to 0.125
- shared_down: bfloat16 [256, 2048], replicated, may hold values from -0.375 to 0.375
- shared_switch: bfloat16 [2048], replicated, may hold values from -0.125 to 0.125
- post_gain: float32 [2048], replicated, may hold values from 0.1 to 1.9
- value_w: bfloat16 [2048, 2048], P('ep'), may hold values from -0.125 to 0.125
- conv_w: float32 [4, 2048], replicated, may hold values from -3 to 3
Outputs:
- expert_mix: bfloat16 [32768, 2048], P(('dp', 'ep')), parts along dimension 0
- value_conv: bfloat16 [32768, 2048], P(('dp', 'ep')), parts along dimension 0
The draws below stay inside these ranges and needn't reach their ends.
There are 4 independent parts, one for each index of `dp`. The reference program is written for one: setup_inputs(seed, part) draws one part's arguments, and reference() takes and returns one part's arrays. A program takes and returns all parts, laid end to end along the dimension named above; an argument that names none is the same for every part. Nothing has to cross between parts.
Inputs may be any that keep to these rules, and one draw needn't show every extreme that they name: `routes`: each row names 10 different experts. Among the 128 rows of one device no expert is named more than 24 times, a bound that some block reaches.
All inputs are finite; a program needn't handle non-finite values.
Results may differ from the reference program's by a relative error of at most 0.0067.
Values may be sent and summed in bfloat16 or wider, within the bound.
A program may use at most 128 MiB of HBM per device.

```python
import math
import jax
import jax.numpy as jnp
import numpy as np
from jax import lax

D = 2048
FF = 512
FF_SH = 256
VCH = 2048
EXPERTS = 64
TOP = 10
KTAP = 4
TOK_DEV = 128
CAP = 24
TOKENS = 8192
N_EP = 64


def shard_levels(rng, extent, cuts, low, top_value):
    def one(position, blocks):
        steps = jax.random.uniform(jax.random.fold_in(jax.random.fold_in(rng, 6), position), (blocks,), jnp.float32, low / len(cuts), top_value / len(cuts))
        return jnp.repeat(jnp.exp(steps), extent[position] // blocks).reshape((-1,) + (1,) * (len(extent) - position - 1))

    factor_of = one(*cuts[0])
    for cut in cuts[1:]:
        factor_of = factor_of * one(*cut)
    return factor_of


def assign_block(rng, own, number, rows, count, top, bound, lean):
    sequence = jax.random.permutation(rng, count)
    packed, common = portions_of(count, rows * top, bound, lean, True), portions_of(count, rows * top, bound, lean, False)
    places = jnp.arange(count)

    def named(tallies, offset_by):
        used = int((tallies > 0).sum())
        fixed = max(1, used // 4)
        moved = fixed + (places - fixed + offset_by * (used - fixed)) % max(1, count - fixed)
        return jnp.zeros((count,), jnp.int32).at[sequence[jnp.where(places < fixed, places, moved)]].set(jnp.asarray(tallies, jnp.int32))

    tallies = jnp.where(number % 4 == 0, named(packed, number // 4), named(common, number - number // 4 - 1))
    mixed = jax.random.permutation(jax.random.fold_in(own, 3), count)
    giver, receiver = mixed[0:count // 2 * 2:2], mixed[1:count // 2 * 2:2]
    room = jnp.minimum(tallies[giver] - 1, bound - tallies[receiver]) // 2
    room = jnp.where((giver == sequence[0]) | (receiver == sequence[0]) | (tallies[receiver] == 0), 0, jnp.maximum(room, 0))
    moved = jax.random.randint(jax.random.fold_in(own, 4), (count // 2,), 0, 1 << 20) % (room + 1)
    tallies = tallies.at[giver].add(-moved).at[receiver].add(moved)
    labels = jnp.searchsorted(jnp.cumsum(tallies), jnp.arange(rows * top), side="right").astype(jnp.int32)
    table = labels.reshape(top, rows).T
    table = table[jax.random.permutation(jax.random.fold_in(own, 1), rows)]
    offset_by = jax.random.randint(jax.random.fold_in(own, 2), (rows, 1), 0, top)
    return jnp.take_along_axis(table, (jnp.arange(top)[None, :] + offset_by) % top, axis=1)


def portions_of(number_of, total, limit, lean, full):
    portions = [(1 << 20) // math.isqrt(rank ** lean) + 1 for rank in range(1, number_of + 1)]
    largest = limit if full else min(limit, max(-(-total // number_of), total * portions[0] // sum(portions)))
    least = 1 if total - largest >= number_of - 1 else 0
    counts, rest = [largest] + [least] * (number_of - 1), total - largest - least * (number_of - 1)
    while rest > 0:
        free = [i for i in range(1, number_of) if counts[i] < largest] or [i for i in range(1, number_of) if counts[i] < limit]
        pool, budget = sum([portions[i] for i in free]), rest
        for i in free:
            addition = min(limit - counts[i], max(1, budget * portions[i] // pool), rest)
            counts[i] = counts[i] + addition
            rest = rest - addition
    return np.array(counts)


def bell_draw(own_key, extent, deviation, bound, split=(), kind=jnp.bfloat16):
    array = deviation * jax.random.normal(own_key, extent, jnp.float32)
    if split:
        array = array * shard_levels(own_key, extent, split, -0.22, 0.18)
    return jnp.clip(array, -bound, bound).astype(kind)


def setup_inputs(seed: int = 0, part: int = 0) -> dict:
    key_of = jax.random.split(jax.random.key(seed), 15)
    own_keys = jax.random.split(jax.random.fold_in(key_of[14], part), 15)
    tokens = bell_draw(own_keys[0], (TOKENS, D), 1.0, 6.0, ((0, 64),))
    routes_keys = jax.random.split(jax.random.fold_in(own_keys[1], 1), TOKENS // TOK_DEV)
    routes_turns = jax.random.permutation(jax.random.fold_in(own_keys[1], 3), TOKENS // TOK_DEV)
    routes = jax.vmap(lambda own, number: assign_block(jax.random.fold_in(own_keys[1], 2), own, number, TOK_DEV, EXPERTS, TOP, CAP, 2))(routes_keys, routes_turns).reshape((TOKENS, TOP))
    gate_share = jnp.clip(jnp.exp(math.log(1.0) - 2.3025851 * jax.random.uniform(own_keys[2], (TOKENS, TOP), jnp.float32) ** shard_levels(own_keys[2], (TOKENS, TOP), ((0, 64),), -0.2, 0.2)), 0.1, 1.0)
    norm_gain = jnp.clip(1.0 + 0.18 * jax.random.normal(key_of[3], (D,), jnp.float32), 0.1, 1.9)
    w_gate = bell_draw(key_of[4], (EXPERTS, D, FF), D ** -0.5, 0.125, ((0, 64),))
    w_up = bell_draw(key_of[5], (EXPERTS, D, FF), D ** -0.5, 0.125, ((0, 64),))
    w_down = bell_draw(key_of[6], (EXPERTS, FF, D), FF ** -0.5, 0.25, ((0, 64),))
    shared_gate = bell_draw(key_of[7], (D, FF_SH), D ** -0.5, 0.125)
    shared_up = bell_draw(key_of[8], (D, FF_SH), D ** -0.5, 0.125)
    shared_down = bell_draw(key_of[9], (FF_SH, D), FF_SH ** -0.5, 0.375)
    shared_switch = bell_draw(key_of[10], (D,), D ** -0.5, 0.125)
    post_gain = jnp.clip(1.0 + 0.18 * jax.random.normal(key_of[11], (D,), jnp.float32), 0.1, 1.9)
    value_w = bell_draw(key_of[12], (D, VCH), D ** -0.5, 0.125, ((0, 64),))
    conv_w = bell_draw(key_of[13], (KTAP, VCH), 0.5, 3.0, (), jnp.float32)
    return dict(tokens=tokens, routes=routes, gate_share=gate_share, norm_gain=norm_gain, w_gate=w_gate, w_up=w_up, w_down=w_down, shared_gate=shared_gate, shared_up=shared_up, shared_down=shared_down, shared_switch=shared_switch, post_gain=post_gain, value_w=value_w, conv_w=conv_w)


def rms_norm(values, gain):
    return values * lax.rsqrt(lax.optimization_barrier(jnp.mean(values * values, axis=-1, keepdims=True)) + 1e-06) * gain

def reference(tokens, routes, gate_share, norm_gain, w_gate, w_up, w_down, shared_gate, shared_up, shared_down, shared_switch, post_gain, value_w, conv_w):
    resid = tokens.astype(jnp.float32)
    normed = rms_norm(resid, norm_gain).astype(jnp.bfloat16)
    shares = gate_share / lax.optimization_barrier(jnp.sum(gate_share, axis=-1, keepdims=True))
    blocks = routes.reshape(N_EP, TOK_DEV * TOP)
    onehot = (blocks[:, :, None] == jnp.arange(EXPERTS, dtype=jnp.int32)[None, None, :]).astype(jnp.int32)
    slot_rank = lax.optimization_barrier(jnp.sum((jnp.cumsum(onehot, axis=1) - onehot) * onehot, axis=-1)).astype(jnp.int32)
    sources = jnp.arange(N_EP, dtype=jnp.int32)[:, None]
    target = (blocks * (N_EP * CAP) + sources * CAP + slot_rank).reshape(-1).astype(jnp.int32)
    token_ids = (jnp.arange(TOKENS * TOP, dtype=jnp.int32) // TOP).astype(jnp.int32)
    row_table = jnp.zeros((EXPERTS * N_EP * CAP,), jnp.int32).at[target].set(token_ids).reshape(EXPERTS, N_EP * CAP)
    weight_table = jnp.zeros((EXPERTS * N_EP * CAP,), jnp.float32).at[target].set(shares.reshape(-1)).reshape(EXPERTS, N_EP * CAP)

    def expert_step(running, member):
        row_ids, row_weight, gate_mat, up_mat, down_mat = member
        picked = normed[row_ids]
        gate_act = jnp.dot(picked, gate_mat, preferred_element_type=jnp.float32)
        up_act = jnp.dot(picked, up_mat, preferred_element_type=jnp.float32)
        hidden = (jax.nn.silu(gate_act) * up_act).astype(jnp.bfloat16)
        output = jnp.dot(hidden, down_mat, preferred_element_type=jnp.float32).astype(jnp.bfloat16)
        running = running.at[row_ids].add(output.astype(jnp.float32) * row_weight[:, None])
        return (running, None)
    routed, unused = lax.scan(expert_step, jnp.zeros((TOKENS, D), jnp.float32), (row_table, weight_table, w_gate, w_up, w_down))
    shared_hidden = (jax.nn.silu(jnp.dot(normed, shared_gate, preferred_element_type=jnp.float32)) * jnp.dot(normed, shared_up, preferred_element_type=jnp.float32)).astype(jnp.bfloat16)
    switch = jax.nn.sigmoid(jnp.dot(normed, shared_switch.reshape(D, 1), preferred_element_type=jnp.float32))
    mixture = routed + switch * jnp.dot(shared_hidden, shared_down, preferred_element_type=jnp.float32)
    expert_mix = mixture.astype(jnp.bfloat16)
    post_normed = rms_norm(resid + mixture, post_gain).astype(jnp.bfloat16)
    values = jnp.dot(post_normed, value_w, preferred_element_type=jnp.float32).astype(jnp.bfloat16)
    padded = jnp.concatenate([jnp.zeros((KTAP - 1, VCH), jnp.float32), values.astype(jnp.float32)], axis=0)
    summed = jnp.zeros((TOKENS, VCH), jnp.float32)
    for tap_index in range(KTAP):
        summed = summed + conv_w[tap_index][None, :] * padded[tap_index:tap_index + TOKENS]
    value_conv = jax.nn.silu(summed).astype(jnp.bfloat16)
    return (expert_mix, value_conv)
```

```python
import functools

import jax
import jax.numpy as jnp
from jax import lax
from jax.experimental import pallas as pl
from jax.experimental.pallas import tpu as pltpu
from jax.sharding import PartitionSpec as P

MESH = pl.DeviceIdType.MESH
F32, BF16 = jnp.float32, jnp.bfloat16
NY, NZ, NP = 4, 8, 8
CAP = 24
T = 128
D = 2048
FF = 512
CT = 512
MiB = 2**20

FAR, OWN, L1, R1, L2, R2, L3, R3 = range(8)
SRC_DIST = (4, 0, 1, 7, 2, 6, 3, 5)
CHUNKS = (
    (16, 0, OWN, 1),
    (48, 128, L1, 2),
    (48, 512, L2, 2),
    (48, 896, L3, 2),
    (32, 1280, FAR, 2),
)
SLOT_ROWS = NP * 192
PEERS = [(dy, dc) for dy in range(NY) for dc in range(2) if (dy, dc) != (0, 0)]


def place_of():
    ep = lax.axis_index("ep")
    return ep // (2 * NZ), lax.rem(ep // 2, NZ), lax.rem(ep, 2)


def device(y, z, c):
    return (y * NZ + z) * 2 + c


def remote(src, dst, send, recv, target):
    return pltpu.make_async_remote_copy(
        src, dst, send, recv, device_id={"ep": target}, device_id_type=MESH
    )


def silu(v):
    return v * (1.0 / (1.0 + jnp.exp(-v)))


def chunk_keys(meta, chunk):
    if chunk == 0:
        return meta[OWN, 0:8, :]
    if chunk == 4:
        own = meta[OWN, 0:8, :]
        own = jnp.where(own >= 16.0, own + 8.0, -1000.0)
        return jnp.concatenate([meta[FAR, 0:8, :], own], axis=1)
    first = CHUNKS[chunk][2]
    return jnp.concatenate([meta[first, 0:8, :], meta[first + 1, 0:8, :] + 24.0], axis=1)


def chunk_shares(meta, chunk):
    first, blocks = CHUNKS[chunk][2:]
    if blocks == 1:
        return meta[first, 8:16, :]
    return jnp.concatenate([meta[first, 8:16, :], meta[first + 1, 8:16, :]], axis=1)


def chunk_matches(meta, chunk):
    rows = CHUNKS[chunk][0]
    keys = chunk_keys(meta, chunk)
    number = lax.broadcasted_iota(jnp.int32, (rows, keys.shape[1]), 0).astype(F32)
    return [keys[p : p + 1, :] == number for p in range(NP)]


def moe_kernel(
    tokens,
    routes_t,
    share_t,
    norm_gain,
    switch_w,
    post_gain,
    w_gate,
    w_up,
    w_down,
    s_gate,
    s_up,
    s_down,
    mix_out,
    post_out,
    xs,
    meta_src,
    meta,
    g,
    r,
    o,
    v,
    hid,
    own,
    rs_send,
    rs_recv,
    wg,
    wu,
    wd,
    sg,
    su,
    sd,
    w_sem,
    ag_send,
    ag_recv,
    meta_send,
    meta_recv,
    y_send,
    y_recv,
    b_send,
    b_recv,
    loc_sem,
    rs_s,
    rs_r,
):
    y, z, c = place_of()
    me = y * 2 + c
    barrier = pltpu.get_barrier_semaphore()
    right = device(y, lax.rem(z + 1, NZ), c)
    left = device(y, lax.rem(z + NZ - 1, NZ), c)

    def peer(dy, dc):
        return lax.rem(y + dy, NY), lax.rem(c + dc, 2)

    for d in range(1, NZ):
        pl.semaphore_signal(
            barrier, 1, device_id={"ep": device(y, lax.rem(z + d, NZ), c)}, device_id_type=MESH
        )
    for dy, dc in PEERS:
        py, pc = peer(dy, dc)
        pl.semaphore_signal(barrier, 1, device_id={"ep": device(py, z, pc)}, device_id_type=MESH)

    loads = [
        pltpu.make_async_copy(a, b, w_sem.at[i])
        for i, (a, b) in enumerate(
            ((s_gate, sg), (s_up, su), (s_down, sd), (w_gate, wg), (w_up, wu), (w_down, wd))
        )
    ]
    for load in loads:
        load.start()

    own_rows = pl.ds(OWN * T, T)
    x = tokens[...].astype(F32)
    scale = lax.rsqrt(jnp.mean(x * x, axis=-1, keepdims=True) + 1e-06)
    xs[own_rows, :] = (x * scale * norm_gain[...]).astype(BF16)

    pl.semaphore_wait(barrier, NZ - 1 + len(PEERS))

    def block(place, first=0, rows=T):
        return xs.at[pl.ds(place * T + first, rows), :]

    def gather_step(i, src, dst, target):
        copy = remote(src, dst, ag_send.at[i], ag_recv.at[i], target)
        copy.start()
        return copy

    ag = [
        gather_step(0, block(OWN), block(L1), right),
        gather_step(1, block(OWN), block(R1), left),
    ]

    row = lax.broadcasted_iota(jnp.int32, (64, T), 0)
    in_col = lax.rem(row, 8)
    expert = (in_col // 2) * (2 * NZ) + (row // 8) * 2 + lax.rem(in_col, 2)
    gate = share_t[...]
    share = gate / jnp.sum(gate, axis=0, keepdims=True)
    named = jnp.zeros((64, T), F32)
    weight = jnp.zeros((64, T), F32)
    for k in range(10):
        hit = routes_t[k : k + 1, :] == expert
        named = named + jnp.where(hit, 1.0, 0.0)
        weight = weight + jnp.where(hit, share[k : k + 1, :], 0.0)
    earlier = lax.broadcasted_iota(jnp.int32, (T, T), 0) < lax.broadcasted_iota(
        jnp.int32, (T, T), 1
    )
    count = jnp.dot(
        named.astype(BF16), jnp.where(earlier, 1.0, 0.0).astype(BF16), preferred_element_type=F32
    )
    slot = jnp.where(named > 0.0, count, -1000.0)
    for col in range(NZ):
        meta_src[col, 0:8, :] = slot[col * 8 : col * 8 + 8, :]
        meta_src[col, 8:16, :] = weight[col * 8 : col * 8 + 8, :]
    meta[OWN] = meta_src[z]
    metas = {}
    for place, d in enumerate(SRC_DIST):
        if d:
            col = lax.rem(z + d, NZ)
            metas[place] = remote(
                meta_src.at[col], meta.at[place], meta_send.at[place], meta_recv.at[place],
                device(y, col, c),
            )
            metas[place].start()

    def peer_rows(chunk, p):
        rows, base = CHUNKS[chunk][:2]
        return pl.ds(pl.multiple_of(base + p * rows, 16), rows)

    def exchange(chunk, src, dst, send, recv, turn):
        copies = []
        for dy, dc in PEERS:
            i = dy * 2 + dc
            py, pc = peer(dy if turn > 0 else (NY - dy) % NY, dc)
            copy = remote(
                src.at[peer_rows(chunk, py * 2 + pc), :],
                dst.at[peer_rows(chunk, me), :],
                send.at[chunk, i],
                recv.at[chunk, i],
                device(py, z, pc),
            )
            copy.start()
            copies.append(copy)
        here = pltpu.make_async_copy(
            src.at[peer_rows(chunk, me), :],
            dst.at[peer_rows(chunk, me), :],
            loc_sem.at[0 if turn > 0 else 1, chunk],
        )
        here.start()
        return copies, here

    def select(chunk):
        rows, base, first, blocks = CHUNKS[chunk]
        pick = jnp.concatenate(
            [jnp.where(m, 1.0, 0.0) for m in chunk_matches(meta, chunk)], axis=0
        ).astype(BF16)

        @pl.loop(0, D // CT)
        def _(i):
            cols = pl.ds(pl.multiple_of(i * CT, CT), CT)
            g[pl.ds(base, NP * rows), cols] = jnp.dot(
                pick, xs[pl.ds(first * T, blocks * T), cols], preferred_element_type=F32
            ).astype(BF16)

        return exchange(chunk, g, r, y_send, y_recv, 1)

    def arrived(sent):
        for copy in sent[0]:
            copy.wait_recv()
        sent[1].wait()

    def run_expert(chunk):
        rows, base = CHUNKS[chunk][:2]
        n = NP * rows
        some = pl.ds(base, n)

        @pl.loop(0, FF // 256)
        def _(i):
            cols = pl.ds(pl.multiple_of(i * 256, 256), 256)
            gate_act = jnp.dot(r[some, :], wg[:, cols], preferred_element_type=F32)
            up_act = jnp.dot(r[some, :], wu[:, cols], preferred_element_type=F32)
            hid[0:n, cols] = (silu(gate_act) * up_act).astype(BF16)

        @pl.loop(0, D // CT)
        def _(i):
            cols = pl.ds(pl.multiple_of(i * CT, CT), CT)
            o[some, cols] = jnp.dot(hid[0:n, :], wd[:, cols], preferred_element_type=F32).astype(
                BF16
            )

    def give_back(chunk):
        return exchange(chunk, o, v, b_send, b_recv, -1)

    def weights_of(chunk):
        shares = chunk_shares(meta, chunk)
        w = jnp.concatenate(
            [
                jnp.where(m, shares[p : p + 1, :], 0.0)
                for p, m in enumerate(chunk_matches(meta, chunk))
            ],
            axis=0,
        )
        high = w.astype(BF16)
        return high, (w - high.astype(F32)).astype(BF16)

    def weigh(chunk, w, cols):
        rows, base = CHUNKS[chunk][:2]
        vals = v[pl.ds(base, NP * rows), cols]
        dims = (((0,), (0,)), ((), ()))
        return lax.dot_general(w[0], vals, dims, preferred_element_type=F32) + lax.dot_general(
            w[1], vals, dims, preferred_element_type=F32
        )

    out = {0: select(0)}

    for load in loads[:3]:
        load.wait()
    n_own = xs[own_rows, :]
    switch_sum = jnp.sum(n_own.astype(F32) * switch_w[...].astype(F32), axis=-1, keepdims=True)
    switch = 1.0 / (1.0 + jnp.exp(-switch_sum))
    shared = (
        silu(jnp.dot(n_own, sg[...], preferred_element_type=F32))
        * jnp.dot(n_own, su[...], preferred_element_type=F32)
    ).astype(BF16)

    @pl.loop(0, D // CT)
    def _(i):
        cols = pl.ds(pl.multiple_of(i * CT, CT), CT)
        own[:, cols] = switch * jnp.dot(shared, sd[:, cols], preferred_element_type=F32)

    ag[0].wait_recv()
    ag.append(gather_step(2, block(L1), block(L2), right))
    ag[1].wait_recv()
    ag.append(gather_step(3, block(R1), block(R2), left))
    metas[L1].wait_recv()
    metas[R1].wait_recv()
    out[1] = select(1)

    ag[2].wait_recv()
    ag.append(gather_step(4, block(L2), block(L3), right))
    ag[3].wait_recv()
    ag.append(gather_step(5, block(R2), block(R3), left))
    metas[L2].wait_recv()
    metas[R2].wait_recv()
    out[2] = select(2)

    for load in loads[3:]:
        load.wait()
    arrived(out[0])
    run_expert(0)

    ag[4].wait_recv()
    ag.append(gather_step(6, block(L3, 0, 64), block(FAR, 0, 64), right))
    ag[5].wait_recv()
    ag.append(gather_step(7, block(R3, 64, 64), block(FAR, 64, 64), left))
    metas[L3].wait_recv()
    metas[R3].wait_recv()
    out[3] = select(3)

    ag[6].wait_recv()
    ag[7].wait_recv()
    metas[FAR].wait_recv()
    out[4] = select(4)

    back = {}
    for chunk in (1, 2, 3):
        arrived(out[chunk])
        run_expert(chunk)
    back[3] = give_back(3)
    arrived(out[4])
    run_expert(4)
    back[4] = give_back(4)
    back[2] = give_back(2)

    def pass_on(i, place, first, rows, target):
        some = pl.ds(place * T + first, rows)
        copy = remote(
            rs_send.at[some, :], rs_recv.at[some, :], rs_s.at[i], rs_r.at[i], target
        )
        copy.start()
        return copy

    w4 = weights_of(4)
    arrived(back[4])

    @pl.loop(0, D // CT)
    def _(i):
        cols = pl.ds(pl.multiple_of(i * CT, CT), CT)
        part = weigh(4, w4, cols)
        rs_send[pl.ds(FAR * T, T), cols] = part[0:T, :].astype(BF16)
        own[:, cols] += part[T:, :]

    rs = [pass_on(0, FAR, 0, 64, left), pass_on(1, FAR, 64, 64, right)]
    back[1] = give_back(1)

    def add_block(chunk, w, got_left, got_right):
        first = CHUNKS[chunk][2]
        got_left = pl.ds(got_left[0], got_left[1])
        got_right = pl.ds(got_right[0], got_right[1])

        @pl.loop(0, D // CT)
        def _(i):
            cols = pl.ds(pl.multiple_of(i * CT, CT), CT)
            part = weigh(chunk, w, cols)
            a = rs_recv[got_left, cols].astype(F32)
            b = rs_recv[got_right, cols].astype(F32)
            if a.shape[0] == 64:
                more = jnp.concatenate([a, jnp.zeros((T, CT), F32), b], axis=0)
            else:
                more = jnp.concatenate([a, b], axis=0)
            rs_send[pl.ds(first * T, 2 * T), cols] = (part + more).astype(BF16)

    w3 = weights_of(3)
    arrived(back[3])
    rs[0].wait_recv()
    rs[1].wait_recv()
    add_block(3, w3, (FAR * T, 64), (FAR * T + 64, 64))
    rs += [pass_on(2, L3, 0, T, left), pass_on(3, R3, 0, T, right)]
    back[0] = give_back(0)

    w2 = weights_of(2)
    arrived(back[2])
    rs[2].wait_recv()
    rs[3].wait_recv()
    add_block(2, w2, (L3 * T, T), (R3 * T, T))
    rs += [pass_on(4, L2, 0, T, left), pass_on(5, R2, 0, T, right)]

    w1 = weights_of(1)
    arrived(back[1])
    rs[4].wait_recv()
    rs[5].wait_recv()
    add_block(1, w1, (L2 * T, T), (R2 * T, T))
    rs += [pass_on(6, L1, 0, T, left), pass_on(7, R1, 0, T, right)]

    w0 = weights_of(0)
    arrived(back[0])

    @pl.loop(0, D // CT)
    def _(i):
        cols = pl.ds(pl.multiple_of(i * CT, CT), CT)
        own[:, cols] += weigh(0, w0, cols)

    rs[6].wait_recv()
    rs[7].wait_recv()
    mixture = (
        own[...]
        + rs_recv[pl.ds(L1 * T, T), :].astype(F32)
        + rs_recv[pl.ds(R1 * T, T), :].astype(F32)
    )
    mix_out[...] = mixture.astype(BF16)
    after = tokens[...].astype(F32) + mixture
    scale = lax.rsqrt(jnp.mean(after * after, axis=-1, keepdims=True) + 1e-06)
    post_out[...] = (after * scale * post_gain[...]).astype(BF16)

    for copy in ag + rs + list(metas.values()):
        copy.wait_send()
    for sent in list(out.values()) + list(back.values()):
        for copy in sent[0]:
            copy.wait_send()


def value_kernel(post, conv_w, value_w, out, vw, wide, tail, got, w_sem, send_sem, recv_sem):
    ep = lax.axis_index("ep")
    n = lax.axis_size("ep")
    barrier = pltpu.get_barrier_semaphore()
    pl.semaphore_signal(
        barrier, 1, device_id={"ep": lax.rem(ep + n - 1, n)}, device_id_type=MESH
    )
    parts = D // CT
    loads = [
        pltpu.make_async_copy(
            value_w.at[:, pl.ds(i * CT, CT)], vw.at[:, pl.ds(i * CT, CT)], w_sem.at[i]
        )
        for i in range(parts)
    ]
    for load in loads:
        load.start()
    rows = post[...]
    for i in range(parts):
        cols = pl.ds(i * CT, CT)
        loads[i].wait()
        vals = jnp.dot(rows, vw[:, cols], preferred_element_type=F32).astype(BF16)
        wide[16 : 16 + T, cols] = vals.astype(F32)
        tail[:, cols] = vals[T - 16 :, :]
    pl.semaphore_wait(barrier, 1)
    copy = remote(tail, got, send_sem, recv_sem, lax.rem(ep + 1, n))
    copy.start()
    copy.wait_recv()
    before = jnp.where(ep > 0, 1.0, 0.0)
    wide[0:16, :] = got[...].astype(F32) * before
    for i in range(parts):
        cols = pl.ds(i * CT, CT)
        total = conv_w[0:1, cols] * wide[13 : 13 + T, cols]
        for j in range(1, 4):
            total = total + conv_w[j : j + 1, cols] * wide[13 + j : 13 + j + T, cols]
        out[:, cols] = silu(total).astype(BF16)
    copy.wait_send()


def local(
    tokens,
    routes,
    gate_share,
    norm_gain,
    w_gate,
    w_up,
    w_down,
    shared_gate,
    shared_up,
    shared_down,
    shared_switch,
    post_gain,
    value_w,
    conv_w,
):
    whole_w = lax.all_gather(value_w, "ep", axis=0, tiled=True)
    routes_t = routes.T
    share_t = gate_share.T
    vmem = pl.BlockSpec(memory_space=pltpu.VMEM)
    hbm = pl.BlockSpec(memory_space=pl.ANY)
    dma = pltpu.SemaphoreType.DMA
    mix, post = pl.pallas_call(
        moe_kernel,
        out_shape=(jax.ShapeDtypeStruct((T, D), BF16), jax.ShapeDtypeStruct((T, D), BF16)),
        in_specs=[vmem] * 6 + [hbm] * 6,
        out_specs=(vmem, vmem),
        scratch_shapes=[
            pltpu.VMEM((8 * T, D), BF16),
            pltpu.VMEM((NZ, 16, T), F32),
            pltpu.VMEM((8, 16, T), F32),
            pltpu.VMEM((SLOT_ROWS, D), BF16),
            pltpu.VMEM((SLOT_ROWS, D), BF16),
            pltpu.VMEM((SLOT_ROWS, D), BF16),
            pltpu.VMEM((SLOT_ROWS, D), BF16),
            pltpu.VMEM((NP * 48, FF), BF16),
            pltpu.VMEM((T, D), F32),
            pltpu.VMEM((8 * T, D), BF16),
            pltpu.VMEM((8 * T, D), BF16),
            pltpu.VMEM((D, FF), BF16),
            pltpu.VMEM((D, FF), BF16),
            pltpu.VMEM((FF, D), BF16),
            pltpu.VMEM(shared_gate.shape, BF16),
            pltpu.VMEM(shared_up.shape, BF16),
            pltpu.VMEM(shared_down.shape, BF16),
            dma((6,)),
            dma((8,)),
            dma((8,)),
            dma((8,)),
            dma((8,)),
            dma((5, 8)),
            dma((5, 8)),
            dma((5, 8)),
            dma((5, 8)),
            dma((2, 5)),
            dma((8,)),
            dma((8,)),
        ],
        compiler_params=pltpu.CompilerParams(
            collective_id=0, has_side_effects=True, vmem_limit_bytes=58 * MiB
        ),
        cost_estimate=pl.CostEstimate(
            flops=12 * 10**9, bytes_accessed=500 * 10**6, transcendentals=0
        ),
        name="experts",
    )(
        tokens,
        routes_t,
        share_t,
        norm_gain.reshape(1, D),
        shared_switch.reshape(1, D),
        post_gain.reshape(1, D),
        w_gate.reshape(D, FF),
        w_up.reshape(D, FF),
        w_down.reshape(FF, D),
        shared_gate,
        shared_up,
        shared_down,
    )
    conv = pl.pallas_call(
        value_kernel,
        out_shape=jax.ShapeDtypeStruct((T, D), BF16),
        in_specs=[vmem, vmem, hbm],
        out_specs=vmem,
        scratch_shapes=[
            pltpu.VMEM((D, D), BF16),
            pltpu.VMEM((16 + T, D), F32),
            pltpu.VMEM((16, D), BF16),
            pltpu.VMEM((16, D), BF16),
            dma((D // CT,)),
            dma,
            dma,
        ],
        compiler_params=pltpu.CompilerParams(
            collective_id=1, has_side_effects=True, vmem_limit_bytes=40 * MiB
        ),
        name="values",
    )(post, conv_w, whole_w)
    return mix, conv


def solution(mesh):
    placed = (
        P(("dp", "ep"), None),
        P(("dp", "ep"), None),
        P(("dp", "ep"), None),
        P(),
        P("ep", None, None),
        P("ep", None, None),
        P("ep", None, None),
        P(),
        P(),
        P(),
        P(),
        P(),
        P("ep", None),
        P(),
    )
    return jax.shard_map(
        local,
        mesh=mesh,
        in_specs=placed,
        out_specs=(P(("dp", "ep"), None), P(("dp", "ep"), None)),
        check_vma=False,
    )
```

```python
import jax
import jax.numpy as jnp
from jax import lax
from jax.experimental import pallas as pl
from jax.experimental.pallas import tpu as pltpu
from jax.sharding import PartitionSpec as P

MESH = pl.DeviceIdType.MESH
F32, BF16 = jnp.float32, jnp.bfloat16
NX, NY, NZ, NP = 4, 4, 8, 8
CAP = 24
T = 128
D = 2048
FF = 512
CT = 512
MiB = 2**20

FAR, OWN, L1, R1, L2, R2, L3, R3 = range(8)
SRC_DIST = (4, 0, 1, 7, 2, 6, 3, 5)
CHUNKS = (
    (16, 0, OWN, 1),
    (48, 128, L1, 2),
    (48, 512, L2, 2),
    (48, 896, L3, 2),
    (32, 1280, FAR, 2),
)
SLOT_ROWS = NP * 192
PEERS = [(dy, dc) for dy in range(NY) for dc in range(2) if (dy, dc) != (0, 0)]


def place_of():
    ep = lax.axis_index("ep")
    return ep // (2 * NZ), lax.rem(ep // 2, NZ), lax.rem(ep, 2)


def device(y, z, c):
    return (y * NZ + z) * 2 + c


def remote(src, dst, send, recv, target):
    return pltpu.make_async_remote_copy(
        src, dst, send, recv, device_id={"ep": target}, device_id_type=MESH
    )


def silu(v):
    return v * (1.0 / (1.0 + jnp.exp(-v)))


def chunk_keys(meta, chunk):
    if chunk == 0:
        return meta[OWN, 0:8, :]
    if chunk == 4:
        own = meta[OWN, 0:8, :]
        own = jnp.where(own >= 16.0, own + 8.0, -1000.0)
        return jnp.concatenate([meta[FAR, 0:8, :], own], axis=1)
    first = CHUNKS[chunk][2]
    return jnp.concatenate([meta[first, 0:8, :], meta[first + 1, 0:8, :] + 24.0], axis=1)


def chunk_shares(meta, chunk):
    first, blocks = CHUNKS[chunk][2:]
    if blocks == 1:
        return meta[first, 8:16, :]
    return jnp.concatenate([meta[first, 8:16, :], meta[first + 1, 8:16, :]], axis=1)


def chunk_matches(meta, chunk):
    rows = CHUNKS[chunk][0]
    keys = chunk_keys(meta, chunk)
    number = lax.broadcasted_iota(jnp.int32, (rows, keys.shape[1]), 0).astype(F32)
    return [keys[p : p + 1, :] == number for p in range(NP)]


def moe_kernel(
    tokens,
    routes_t,
    share_t,
    norm_gain,
    switch_w,
    post_gain,
    conv_w,
    w_gate,
    w_up,
    w_down,
    s_gate,
    s_up,
    s_down,
    value_w,
    mix_out,
    conv_out,
    xs,
    meta_src,
    meta,
    g,
    r,
    v,
    hid,
    own,
    rs_recv,
    wg,
    wu,
    wd,
    sg,
    su,
    sd,
    vw,
    wide,
    tail,
    got,
    w_sem,
    ag_send,
    ag_recv,
    meta_send,
    meta_recv,
    y_send,
    y_recv,
    b_send,
    b_recv,
    loc_sem,
    rs_s,
    rs_r,
    vy_send,
    vy_recv,
    vz_send,
    vz_recv,
    vx_send,
    vx_recv,
    halo_send,
    halo_recv,
):
    o, rs_send = g, xs
    x_at, ep, n_ep = lax.axis_index("dp"), lax.axis_index("ep"), 2 * NY * NZ
    y, z, c = place_of()
    me = y * 2 + c
    barrier = pltpu.get_barrier_semaphore()
    right = device(y, lax.rem(z + 1, NZ), c)
    left = device(y, lax.rem(z + NZ - 1, NZ), c)

    def peer(dy, dc):
        return lax.rem(y + dy, NY), lax.rem(c + dc, 2)

    for d in range(1, NZ):
        pl.semaphore_signal(
            barrier, 1, device_id={"ep": device(y, lax.rem(z + d, NZ), c)}, device_id_type=MESH
        )
    for dy, dc in PEERS:
        py, pc = peer(dy, dc)
        pl.semaphore_signal(barrier, 1, device_id={"ep": device(py, z, pc)}, device_id_type=MESH)
    for dx in range(1, NX):
        pl.semaphore_signal(
            barrier, 1, device_id={"dp": lax.rem(x_at + dx, NX), "ep": ep}, device_id_type=MESH
        )
    pl.semaphore_signal(
        barrier, 1, device_id={"ep": lax.rem(ep + n_ep - 1, n_ep)}, device_id_type=MESH
    )

    loads = [
        pltpu.make_async_copy(a, b, w_sem.at[i])
        for i, (a, b) in enumerate(
            ((s_gate, sg), (s_up, su), (s_down, sd), (w_gate, wg), (w_up, wu), (w_down, wd))
        )
    ]
    for load in loads:
        load.start()
    quarter = pl.ds(pl.multiple_of(x_at * (D // NX), D // NX), D // NX)
    value_own = pltpu.make_async_copy(
        value_w.at[:, quarter], vw.at[y, z, c, :, quarter], w_sem.at[6]
    )
    value_own.start()

    own_rows = pl.ds(OWN * T, T)
    resid = tokens[...].astype(F32)
    scale = lax.rsqrt(jnp.mean(resid * resid, axis=-1, keepdims=True) + 1e-06)
    xs[own_rows, :] = (resid * scale * norm_gain[...]).astype(BF16)

    pl.semaphore_wait(barrier, NZ - 1 + len(PEERS) + NX - 1 + 1)

    def block(place, first=0, rows=T):
        return xs.at[pl.ds(place * T + first, rows), :]

    def gather_step(i, src, dst, target):
        copy = remote(src, dst, ag_send.at[i], ag_recv.at[i], target)
        copy.start()
        return copy

    ag = [
        gather_step(0, block(OWN), block(L1), right),
        gather_step(1, block(OWN), block(R1), left),
    ]

    row = lax.broadcasted_iota(jnp.int32, (64, T), 0)
    in_col = lax.rem(row, 8)
    expert = (in_col // 2) * (2 * NZ) + (row // 8) * 2 + lax.rem(in_col, 2)
    gate = share_t[...]
    share = gate / jnp.sum(gate, axis=0, keepdims=True)
    named = jnp.zeros((64, T), F32)
    weight = jnp.zeros((64, T), F32)
    for k in range(10):
        hit = routes_t[k : k + 1, :] == expert
        named = named + jnp.where(hit, 1.0, 0.0)
        weight = weight + jnp.where(hit, share[k : k + 1, :], 0.0)
    earlier = lax.broadcasted_iota(jnp.int32, (T, T), 0) < lax.broadcasted_iota(
        jnp.int32, (T, T), 1
    )
    count = jnp.dot(
        named.astype(BF16), jnp.where(earlier, 1.0, 0.0).astype(BF16), preferred_element_type=F32
    )
    slot = jnp.where(named > 0.0, count, -1000.0)
    for col in range(NZ):
        meta_src[col, 0:8, :] = slot[col * 8 : col * 8 + 8, :]
        meta_src[col, 8:16, :] = weight[col * 8 : col * 8 + 8, :]
    meta[OWN] = meta_src[z]
    metas = {}
    for place, d in enumerate(SRC_DIST):
        if d:
            col = lax.rem(z + d, NZ)
            metas[place] = remote(
                meta_src.at[col], meta.at[place], meta_send.at[place], meta_recv.at[place],
                device(y, col, c),
            )
            metas[place].start()

    def peer_rows(chunk, p):
        rows, base = CHUNKS[chunk][:2]
        return pl.ds(pl.multiple_of(base + p * rows, 16), rows)

    def exchange(chunk, src, dst, send, recv, turn):
        copies = []
        for dy, dc in PEERS:
            i = dy * 2 + dc
            py, pc = peer(dy if turn > 0 else (NY - dy) % NY, dc)
            copy = remote(
                src.at[peer_rows(chunk, py * 2 + pc), :],
                dst.at[peer_rows(chunk, me), :],
                send.at[chunk, i],
                recv.at[chunk, i],
                device(py, z, pc),
            )
            copy.start()
            copies.append(copy)
        here = pltpu.make_async_copy(
            src.at[peer_rows(chunk, me), :],
            dst.at[peer_rows(chunk, me), :],
            loc_sem.at[0 if turn > 0 else 1, chunk],
        )
        here.start()
        return copies, here

    def select(chunk):
        rows, base, first, blocks = CHUNKS[chunk]
        pick = jnp.concatenate(
            [jnp.where(m, 1.0, 0.0) for m in chunk_matches(meta, chunk)], axis=0
        ).astype(BF16)

        @pl.loop(0, D // CT)
        def _(i):
            cols = pl.ds(pl.multiple_of(i * CT, CT), CT)
            g[pl.ds(base, NP * rows), cols] = jnp.dot(
                pick, xs[pl.ds(first * T, blocks * T), cols], preferred_element_type=F32
            ).astype(BF16)

        return exchange(chunk, g, r, y_send, y_recv, 1)

    def arrived(sent):
        for copy in sent[0]:
            copy.wait_recv()
        sent[1].wait()

    def run_expert(chunk):
        rows, base = CHUNKS[chunk][:2]
        for copy in out[chunk][0]:
            copy.wait_send()
        n = NP * rows
        some = pl.ds(base, n)

        @pl.loop(0, FF // 256)
        def _(i):
            cols = pl.ds(pl.multiple_of(i * 256, 256), 256)
            gate_act = jnp.dot(r[some, :], wg[:, cols], preferred_element_type=F32)
            up_act = jnp.dot(r[some, :], wu[:, cols], preferred_element_type=F32)
            hid[0:n, cols] = (silu(gate_act) * up_act).astype(BF16)

        @pl.loop(0, D // CT)
        def _(i):
            cols = pl.ds(pl.multiple_of(i * CT, CT), CT)
            o[some, cols] = jnp.dot(hid[0:n, :], wd[:, cols], preferred_element_type=F32).astype(
                BF16
            )

    def give_back(chunk):
        return exchange(chunk, o, v, b_send, b_recv, -1)

    def weights_of(chunk):
        shares = chunk_shares(meta, chunk)
        w = jnp.concatenate(
            [
                jnp.where(m, shares[p : p + 1, :], 0.0)
                for p, m in enumerate(chunk_matches(meta, chunk))
            ],
            axis=0,
        )
        high = w.astype(BF16)
        return high, (w - high.astype(F32)).astype(BF16)

    def weigh(chunk, w, cols):
        rows, base = CHUNKS[chunk][:2]
        vals = v[pl.ds(base, NP * rows), cols]
        dims = (((0,), (0,)), ((), ()))
        return lax.dot_general(w[0], vals, dims, preferred_element_type=F32) + lax.dot_general(
            w[1], vals, dims, preferred_element_type=F32
        )

    out = {0: select(0)}
    by_y = []
    for dy in range(1, NY):
        by_y.append(
            remote(
                value_w.at[:, quarter], vw.at[y, z, c, :, quarter], vy_send.at[dy], vy_recv.at[dy],
                device(lax.rem(y + dy, NY), z, c),
            )
        )
        by_y[-1].start()

    for load in loads[:3]:
        load.wait()
    n_own = xs[own_rows, :]
    switch_sum = jnp.zeros((T, 128), F32)
    switch_row = switch_w[...].astype(F32)
    for i in range(D // 128):
        part = xs[own_rows, pl.ds(i * 128, 128)].astype(F32)
        switch_sum = switch_sum + part * switch_row[i : i + 1, :]
    switch_sum = jnp.sum(switch_sum, axis=-1, keepdims=True)
    switch = 1.0 / (1.0 + jnp.exp(-switch_sum))
    shared = (
        silu(jnp.dot(n_own, sg[...], preferred_element_type=F32))
        * jnp.dot(n_own, su[...], preferred_element_type=F32)
    ).astype(BF16)

    @pl.loop(0, D // CT)
    def _(i):
        cols = pl.ds(pl.multiple_of(i * CT, CT), CT)
        own[:, cols] = switch * jnp.dot(shared, sd[:, cols], preferred_element_type=F32)

    ag[0].wait_recv()
    ag.append(gather_step(2, block(L1), block(L2), right))
    ag[1].wait_recv()
    ag.append(gather_step(3, block(R1), block(R2), left))
    metas[L1].wait_recv()
    metas[R1].wait_recv()
    out[1] = select(1)

    ag[2].wait_recv()
    ag.append(gather_step(4, block(L2), block(L3), right))
    ag[3].wait_recv()
    ag.append(gather_step(5, block(R2), block(R3), left))
    metas[L2].wait_recv()
    metas[R2].wait_recv()
    out[2] = select(2)

    for load in loads[3:]:
        load.wait()
    arrived(out[0])
    run_expert(0)

    ag[4].wait_recv()
    ag.append(gather_step(6, block(L3, 0, 64), block(FAR, 0, 64), right))
    ag[5].wait_recv()
    ag.append(gather_step(7, block(R3, 64, 64), block(FAR, 64, 64), left))
    metas[L3].wait_recv()
    metas[R3].wait_recv()
    out[3] = select(3)

    value_own.wait()
    for copy in by_y:
        copy.wait_recv()
    by_z = []
    for d in range(1, NZ):
        part = vw.at[:, z, c, :, quarter]
        by_z.append(
            remote(
                part, part, vz_send.at[d], vz_recv.at[d], device(y, lax.rem(z + d, NZ), c)
            )
        )
        by_z[-1].start()

    ag[6].wait_recv()
    ag[7].wait_recv()
    metas[FAR].wait_recv()
    out[4] = select(4)

    back = {}
    for chunk in (1, 2, 3):
        arrived(out[chunk])
        run_expert(chunk)
    back[3] = give_back(3)
    for copy in by_z:
        copy.wait_recv()
    by_x = []
    for dx in range(1, NX):
        part = vw.at[:, :, c, :, quarter]
        copy = pltpu.make_async_remote_copy(
            part, part, vx_send.at[dx], vx_recv.at[dx],
            device_id={"dp": lax.rem(x_at + dx, NX), "ep": ep}, device_id_type=MESH,
        )
        copy.start()
        by_x.append(copy)
    arrived(out[4])
    run_expert(4)
    back[4] = give_back(4)
    back[2] = give_back(2)

    def pass_on(i, place, first, rows, target):
        some = pl.ds(place * T + first, rows)
        copy = remote(
            rs_send.at[some, :], rs_recv.at[some, :], rs_s.at[i], rs_r.at[i], target
        )
        copy.start()
        return copy

    w4 = weights_of(4)
    arrived(back[4])
    for copy in ag:
        copy.wait_send()

    @pl.loop(0, D // CT)
    def _(i):
        cols = pl.ds(pl.multiple_of(i * CT, CT), CT)
        part = weigh(4, w4, cols)
        rs_send[pl.ds(FAR * T, T), cols] = part[0:T, :].astype(BF16)
        own[:, cols] += part[T:, :]

    rs = [pass_on(0, FAR, 0, 64, left), pass_on(1, FAR, 64, 64, right)]
    back[1] = give_back(1)

    def add_block(chunk, w, got_left, got_right):
        first = CHUNKS[chunk][2]
        got_left = pl.ds(got_left[0], got_left[1])
        got_right = pl.ds(got_right[0], got_right[1])

        @pl.loop(0, D // CT)
        def _(i):
            cols = pl.ds(pl.multiple_of(i * CT, CT), CT)
            part = weigh(chunk, w, cols)
            a = rs_recv[got_left, cols].astype(F32)
            b = rs_recv[got_right, cols].astype(F32)
            if a.shape[0] == 64:
                more = jnp.concatenate([a, jnp.zeros((T, CT), F32), b], axis=0)
            else:
                more = jnp.concatenate([a, b], axis=0)
            rs_send[pl.ds(first * T, 2 * T), cols] = (part + more).astype(BF16)

    w3 = weights_of(3)
    arrived(back[3])
    rs[0].wait_recv()
    rs[1].wait_recv()
    add_block(3, w3, (FAR * T, 64), (FAR * T + 64, 64))
    rs += [pass_on(2, L3, 0, T, left), pass_on(3, R3, 0, T, right)]
    back[0] = give_back(0)

    w2 = weights_of(2)
    arrived(back[2])
    rs[2].wait_recv()
    rs[3].wait_recv()
    add_block(2, w2, (L3 * T, T), (R3 * T, T))
    rs += [pass_on(4, L2, 0, T, left), pass_on(5, R2, 0, T, right)]

    for copy in by_x:
        copy.wait_recv()
    part = vw.at[:, :, c, :, :]
    by_core = remote(part, part, vx_send.at[0], vx_recv.at[0], device(y, z, 1 - c))
    by_core.start()

    w1 = weights_of(1)
    arrived(back[1])
    rs[4].wait_recv()
    rs[5].wait_recv()
    add_block(1, w1, (L2 * T, T), (R2 * T, T))
    rs += [pass_on(6, L1, 0, T, left), pass_on(7, R1, 0, T, right)]

    w0 = weights_of(0)
    arrived(back[0])

    @pl.loop(0, D // CT)
    def _(i):
        cols = pl.ds(pl.multiple_of(i * CT, CT), CT)
        own[:, cols] += weigh(0, w0, cols)

    rs[6].wait_recv()
    rs[7].wait_recv()
    mixture = (
        own[...]
        + rs_recv[pl.ds(L1 * T, T), :].astype(F32)
        + rs_recv[pl.ds(R1 * T, T), :].astype(F32)
    )
    mix_out[...] = mixture.astype(BF16)
    after = tokens[...].astype(F32) + mixture
    scale = lax.rsqrt(jnp.mean(after * after, axis=-1, keepdims=True) + 1e-06)
    xs[own_rows, :] = (after * scale * post_gain[...]).astype(BF16)

    by_core.wait_recv()

    def convolve(cols, first, rows):
        total = conv_w[0:1, cols] * wide[first + 13 : first + 13 + rows, cols]
        for j in range(1, 4):
            total = total + conv_w[j : j + 1, cols] * wide[first + 13 + j : first + 13 + j + rows, cols]
        conv_out[first : first + rows, cols] = silu(total).astype(BF16)

    halo = []
    for i in range(D // CT):
        cols = pl.ds(i * CT, CT)
        vals = jnp.dot(
            xs[own_rows, :], vw[:, :, :, :, cols].reshape(D, CT), preferred_element_type=F32
        ).astype(BF16)
        tail[:, cols] = vals[T - 16 :, :]
        halo.append(
            remote(
                tail.at[:, cols], got.at[:, cols], halo_send.at[i], halo_recv.at[i],
                lax.rem(ep + 1, n_ep),
            )
        )
        halo[-1].start()
        wide[16 : 16 + T, cols] = vals.astype(F32)
        convolve(cols, 16, T - 16)
    before = jnp.where(ep > 0, 1.0, 0.0)
    for i in range(D // CT):
        cols = pl.ds(i * CT, CT)
        halo[i].wait_recv()
        wide[0:16, cols] = got[:, cols].astype(F32) * before
        convolve(cols, 0, 16)

    for copy in rs + list(metas.values()) + by_y + by_z + by_x + [by_core] + halo:
        copy.wait_send()
    for sent in back.values():
        for copy in sent[0]:
            copy.wait_send()


def local(
    tokens,
    routes,
    gate_share,
    norm_gain,
    w_gate,
    w_up,
    w_down,
    shared_gate,
    shared_up,
    shared_down,
    shared_switch,
    post_gain,
    value_w,
    conv_w,
):
    routes_t = routes.T
    share_t = gate_share.T
    vmem = pl.BlockSpec(memory_space=pltpu.VMEM)
    hbm = pl.BlockSpec(memory_space=pl.ANY)
    dma = pltpu.SemaphoreType.DMA
    return pl.pallas_call(
        moe_kernel,
        out_shape=(jax.ShapeDtypeStruct((T, D), BF16), jax.ShapeDtypeStruct((T, D), BF16)),
        in_specs=[vmem] * 7 + [hbm] * 7,
        out_specs=(vmem, vmem),
        scratch_shapes=[
            pltpu.VMEM((8 * T, D), BF16),
            pltpu.VMEM((NZ, 16, T), F32),
            pltpu.VMEM((8, 16, T), F32),
            pltpu.VMEM((SLOT_ROWS, D), BF16),
            pltpu.VMEM((SLOT_ROWS, D), BF16),
            pltpu.VMEM((SLOT_ROWS, D), BF16),
            pltpu.VMEM((NP * 48, FF), BF16),
            pltpu.VMEM((T, D), F32),
            pltpu.VMEM((8 * T, D), BF16),
            pltpu.VMEM((D, FF), BF16),
            pltpu.VMEM((D, FF), BF16),
            pltpu.VMEM((FF, D), BF16),
            pltpu.VMEM(shared_gate.shape, BF16),
            pltpu.VMEM(shared_up.shape, BF16),
            pltpu.VMEM(shared_down.shape, BF16),
            pltpu.VMEM((NY, NZ, 2, 32, D), BF16),
            pltpu.VMEM((16 + T, D), F32),
            pltpu.VMEM((16, D), BF16),
            pltpu.VMEM((16, D), BF16),
            dma((7,)),
            dma((8,)),
            dma((8,)),
            dma((8,)),
            dma((8,)),
            dma((5, 8)),
            dma((5, 8)),
            dma((5, 8)),
            dma((5, 8)),
            dma((2, 5)),
            dma((8,)),
            dma((8,)),
            dma((4,)),
            dma((4,)),
            dma((8,)),
            dma((8,)),
            dma((4,)),
            dma((4,)),
            dma((4,)),
            dma((4,)),
        ],
        compiler_params=pltpu.CompilerParams(
            collective_id=0, has_side_effects=True, vmem_limit_bytes=60 * MiB
        ),
        cost_estimate=pl.CostEstimate(
            flops=13 * 10**9, bytes_accessed=500 * 10**6, transcendentals=0
        ),
        name="experts",
    )(
        tokens,
        routes_t,
        share_t,
        norm_gain.reshape(1, D),
        shared_switch.reshape(D // 128, 128),
        post_gain.reshape(1, D),
        conv_w,
        w_gate.reshape(D, FF),
        w_up.reshape(D, FF),
        w_down.reshape(FF, D),
        shared_gate,
        shared_up,
        shared_down,
        value_w,
    )


def solution(mesh):
    placed = (
        P(("dp", "ep"), None),
        P(("dp", "ep"), None),
        P(("dp", "ep"), None),
        P(),
        P("ep", None, None),
        P("ep", None, None),
        P("ep", None, None),
        P(),
        P(),
        P(),
        P(),
        P(),
        P("ep", None),
        P(),
    )
    return jax.shard_map(
        local,
        mesh=mesh,
        in_specs=placed,
        out_specs=(P(("dp", "ep"), None), P(("dp", "ep"), None)),
        check_vma=False,
    )
```

```python
import jax
import jax.numpy as jnp
from jax import lax
from jax.experimental import pallas as pl
from jax.experimental.pallas import tpu as pltpu
from jax.sharding import PartitionSpec as P

MESH = pl.DeviceIdType.MESH
F32, BF16 = jnp.float32, jnp.bfloat16
NX, NY, NZ, NP = 4, 4, 8, 8
CAP = 24
T = 128
D = 2048
FF = 512
CT = 512
HALF = D // 2
MiB = 2**20

FAR, OWN, L1, R1, L2, R2, L3, R3 = range(8)
SRC_DIST = (4, 0, 1, 7, 2, 6, 3, 5)
CHUNKS = (
    (16, 0, OWN, 1),
    (48, 128, L1, 2),
    (48, 512, L2, 2),
    (48, 896, L3, 2),
    (32, 1280, FAR, 2),
)
SLOT_ROWS = NP * 192
ORDER = [(0, 0), (0, 1), (1, 0), (1, 1), (3, 0), (3, 1), (2, 0), (2, 1)]
PEERS = ORDER[1:]
NEAR = 6


def place_of():
    ep = lax.axis_index("ep")
    return ep // (2 * NZ), lax.rem(ep // 2, NZ), lax.rem(ep, 2)


def device(y, z, c):
    return (y * NZ + z) * 2 + c


def remote(src, dst, send, recv, target):
    return pltpu.make_async_remote_copy(
        src, dst, send, recv, device_id={"ep": target}, device_id_type=MESH
    )


def silu(v):
    return v * (1.0 / (1.0 + jnp.exp(-v)))


def chunk_keys(meta, chunk):
    if chunk == 0:
        return meta[OWN, 0:8, :]
    if chunk == 4:
        own = meta[OWN, 0:8, :]
        own = jnp.where(own >= 16.0, own + 8.0, -1000.0)
        return jnp.concatenate([meta[FAR, 0:8, :], own], axis=1)
    first = CHUNKS[chunk][2]
    return jnp.concatenate([meta[first, 0:8, :], meta[first + 1, 0:8, :] + 24.0], axis=1)


def chunk_shares(meta, chunk):
    first, blocks = CHUNKS[chunk][2:]
    if blocks == 1:
        return meta[first, 8:16, :]
    return jnp.concatenate([meta[first, 8:16, :], meta[first + 1, 8:16, :]], axis=1)


def chunk_matches(meta, chunk):
    rows = CHUNKS[chunk][0]
    keys = chunk_keys(meta, chunk)
    number = lax.broadcasted_iota(jnp.int32, (rows, keys.shape[1]), 0).astype(F32)
    return [keys[p : p + 1, :] == number for p in range(NP)]


def moe_kernel(
    tokens,
    routes_t,
    share_t,
    norm_gain,
    switch_w,
    post_gain,
    conv_w,
    w_gate,
    w_up,
    w_down,
    s_gate,
    s_up,
    s_down,
    value_w,
    mix_out,
    conv_out,
    xs,
    meta_src,
    meta,
    g,
    r,
    v,
    hid,
    own,
    rs_recv,
    wg,
    wu,
    wd,
    sg,
    su,
    sd,
    vw,
    wd2,
    far_hid,
    wide,
    tail,
    got,
    w_sem,
    ag_send,
    ag_recv,
    meta_send,
    meta_recv,
    y_send,
    y_recv,
    b_send,
    b_recv,
    loc_sem,
    rs_s,
    rs_r,
    vy_send,
    vy_recv,
    vz_send,
    vz_recv,
    vx_send,
    vx_recv,
    halo_send,
    halo_recv,
    d_send,
    d_recv,
):
    o, rs_send = g, xs
    x_at, ep, n_ep = lax.axis_index("dp"), lax.axis_index("ep"), 2 * NY * NZ
    y, z, c = place_of()
    me = y * 2 + c
    barrier = pltpu.get_barrier_semaphore()
    right = device(y, lax.rem(z + 1, NZ), c)
    left = device(y, lax.rem(z + NZ - 1, NZ), c)

    def peer(dy, dc):
        return lax.rem(y + dy, NY), lax.rem(c + dc, 2)

    for d in range(1, NZ):
        pl.semaphore_signal(
            barrier, 1, device_id={"ep": device(y, lax.rem(z + d, NZ), c)}, device_id_type=MESH
        )
    for dy, dc in PEERS:
        py, pc = peer(dy, dc)
        pl.semaphore_signal(barrier, 1, device_id={"ep": device(py, z, pc)}, device_id_type=MESH)
    for dx in range(1, NX):
        pl.semaphore_signal(
            barrier, 1, device_id={"dp": lax.rem(x_at + dx, NX), "ep": ep}, device_id_type=MESH
        )
    pl.semaphore_signal(
        barrier, 1, device_id={"ep": lax.rem(ep + n_ep - 1, n_ep)}, device_id_type=MESH
    )

    loads = [
        pltpu.make_async_copy(a, b, w_sem.at[i])
        for i, (a, b) in enumerate(
            ((s_gate, sg), (s_up, su), (s_down, sd), (w_gate, wg), (w_up, wu), (w_down, wd))
        )
    ]
    for load in loads:
        load.start()
    quarter = pl.ds(pl.multiple_of(x_at * (D // NX), D // NX), D // NX)
    value_own = pltpu.make_async_copy(
        value_w.at[:, quarter], vw.at[y, z, c, :, quarter], w_sem.at[6]
    )
    value_own.start()

    own_rows = pl.ds(OWN * T, T)
    resid = tokens[...].astype(F32)
    scale = lax.rsqrt(jnp.mean(resid * resid, axis=-1, keepdims=True) + 1e-06)
    xs[own_rows, :] = (resid * scale * norm_gain[...]).astype(BF16)

    pl.semaphore_wait(barrier, NZ - 1 + len(PEERS) + NX - 1 + 1)

    def block(place, first=0, rows=T):
        return xs.at[pl.ds(place * T + first, rows), :]

    def gather_step(i, src, dst, target):
        copy = remote(src, dst, ag_send.at[i], ag_recv.at[i], target)
        copy.start()
        return copy

    ag = [
        gather_step(0, block(OWN), block(L1), right),
        gather_step(1, block(OWN), block(R1), left),
    ]

    row = lax.broadcasted_iota(jnp.int32, (64, T), 0)
    in_col = lax.rem(row, 8)
    expert = (in_col // 2) * (2 * NZ) + (row // 8) * 2 + lax.rem(in_col, 2)
    gate = share_t[...]
    share = gate / jnp.sum(gate, axis=0, keepdims=True)
    named = jnp.zeros((64, T), F32)
    weight = jnp.zeros((64, T), F32)
    for k in range(10):
        hit = routes_t[k : k + 1, :] == expert
        named = named + jnp.where(hit, 1.0, 0.0)
        weight = weight + jnp.where(hit, share[k : k + 1, :], 0.0)
    earlier = lax.broadcasted_iota(jnp.int32, (T, T), 0) < lax.broadcasted_iota(
        jnp.int32, (T, T), 1
    )
    count = jnp.dot(
        named.astype(BF16), jnp.where(earlier, 1.0, 0.0).astype(BF16), preferred_element_type=F32
    )
    slot = jnp.where(named > 0.0, count, -1000.0)
    for col in range(NZ):
        meta_src[col, 0:8, :] = slot[col * 8 : col * 8 + 8, :]
        meta_src[col, 8:16, :] = weight[col * 8 : col * 8 + 8, :]
    meta[OWN] = meta_src[z]
    metas = {}
    for place, d in enumerate(SRC_DIST):
        if d:
            col = lax.rem(z + d, NZ)
            metas[place] = remote(
                meta_src.at[col], meta.at[place], meta_send.at[place], meta_recv.at[place],
                device(y, col, c),
            )
            metas[place].start()

    def peer_rows(chunk, p):
        rows, base = CHUNKS[chunk][:2]
        return pl.ds(pl.multiple_of(base + p * rows, 16), rows)

    def order_rows(chunk, q, n=1):
        rows, base = CHUNKS[chunk][:2]
        return pl.ds(base + q * rows, n * rows)

    def send_out(chunk):
        copies = []
        for q, (dy, dc) in enumerate(ORDER):
            py, pc = peer(dy, dc)
            src = g.at[peer_rows(chunk, py * 2 + pc), :]
            dst = r.at[order_rows(chunk, q), :]
            if q:
                copies.append(
                    remote(src, dst, y_send.at[chunk, q], y_recv.at[chunk, q], device(py, z, pc))
                )
            else:
                here = pltpu.make_async_copy(src, dst, loc_sem.at[0, chunk])
        for copy in copies:
            copy.start()
        here.start()
        return copies, here

    def far_rows(chunk):
        rows, base = CHUNKS[chunk][:2]
        return pl.ds(base // NP, rows)

    def give_back(chunk):
        copies = []
        for q, (dy, dc) in enumerate(ORDER):
            py, pc = peer((NY - dy) % NY, dc)
            if q < NEAR:
                src, dst = o.at[order_rows(chunk, q), :], v.at[peer_rows(chunk, me), :]
            else:
                src, dst = hid.at[order_rows(chunk, q), :], far_hid.at[c, far_rows(chunk), :]
            if q:
                copies.append(
                    remote(src, dst, b_send.at[chunk, q], b_recv.at[chunk, q], device(py, z, pc))
                )
            else:
                here = pltpu.make_async_copy(src, dst, loc_sem.at[1, chunk])
        for copy in copies[::-1]:
            copy.start()
        here.start()
        return copies, here

    def select(chunk):
        rows, base, first, blocks = CHUNKS[chunk]
        pick = jnp.concatenate(
            [jnp.where(m, 1.0, 0.0) for m in chunk_matches(meta, chunk)], axis=0
        ).astype(BF16)

        @pl.loop(0, D // CT)
        def _(i):
            cols = pl.ds(pl.multiple_of(i * CT, CT), CT)
            g[pl.ds(base, NP * rows), cols] = jnp.dot(
                pick, xs[pl.ds(first * T, blocks * T), cols], preferred_element_type=F32
            ).astype(BF16)

        return send_out(chunk)

    def arrived(sent):
        for copy in sent[0]:
            copy.wait_recv()
        sent[1].wait()

    def run_expert(chunk):
        rows, base = CHUNKS[chunk][:2]
        for copy in out[chunk][0]:
            copy.wait_send()
        some = order_rows(chunk, 0, NP)
        near = order_rows(chunk, 0, NEAR)

        @pl.loop(0, FF // 256)
        def _(i):
            cols = pl.ds(pl.multiple_of(i * 256, 256), 256)
            gate_act = jnp.dot(r[some, :], wg[:, cols], preferred_element_type=F32)
            up_act = jnp.dot(r[some, :], wu[:, cols], preferred_element_type=F32)
            hid[some, cols] = (silu(gate_act) * up_act).astype(BF16)

        @pl.loop(0, D // CT)
        def _(i):
            cols = pl.ds(pl.multiple_of(i * CT, CT), CT)
            o[near, cols] = jnp.dot(hid[near, :], wd[:, cols], preferred_element_type=F32).astype(
                BF16
            )

    def returned(chunk):
        copies, here = back[chunk]
        for copy in copies[NEAR - 1 :]:
            copy.wait_recv()
        py = lax.rem(y + 2, NY)

        @pl.loop(0, D // CT)
        def _(i):
            cols = pl.ds(pl.multiple_of(i * CT, CT), CT)
            for e in range(2):
                v[peer_rows(chunk, py * 2 + e), cols] = jnp.dot(
                    far_hid[e, far_rows(chunk), :], wd2[e, :, cols], preferred_element_type=F32
                ).astype(BF16)

        for copy in copies[: NEAR - 1]:
            copy.wait_recv()
        here.wait()

    def weights_of(chunk):
        shares = chunk_shares(meta, chunk)
        w = jnp.concatenate(
            [
                jnp.where(m, shares[p : p + 1, :], 0.0)
                for p, m in enumerate(chunk_matches(meta, chunk))
            ],
            axis=0,
        )
        high = w.astype(BF16)
        return high, (w - high.astype(F32)).astype(BF16)

    def weigh(chunk, w, cols):
        rows, base = CHUNKS[chunk][:2]
        vals = v[pl.ds(base, NP * rows), cols]
        dims = (((0,), (0,)), ((), ()))
        return lax.dot_general(w[0], vals, dims, preferred_element_type=F32) + lax.dot_general(
            w[1], vals, dims, preferred_element_type=F32
        )

    out = {0: select(0)}
    down_y = remote(
        w_down.at[:, quarter], wd2.at[c, :, quarter], d_send.at[0], d_recv.at[0],
        device(lax.rem(y + 2, NY), z, c),
    )
    down_y.start()
    by_y = []
    for dy in range(1, NY):
        by_y.append(
            remote(
                value_w.at[:, quarter], vw.at[y, z, c, :, quarter], vy_send.at[dy], vy_recv.at[dy],
                device(lax.rem(y + dy, NY), z, c),
            )
        )
        by_y[-1].start()

    for load in loads[:3]:
        load.wait()
    n_own = xs[own_rows, :]
    switch_sum = jnp.zeros((T, 128), F32)
    switch_row = switch_w[...].astype(F32)
    for i in range(D // 128):
        part = xs[own_rows, pl.ds(i * 128, 128)].astype(F32)
        switch_sum = switch_sum + part * switch_row[i : i + 1, :]
    switch_sum = jnp.sum(switch_sum, axis=-1, keepdims=True)
    switch = 1.0 / (1.0 + jnp.exp(-switch_sum))
    shared = (
        silu(jnp.dot(n_own, sg[...], preferred_element_type=F32))
        * jnp.dot(n_own, su[...], preferred_element_type=F32)
    ).astype(BF16)

    @pl.loop(0, D // CT)
    def _(i):
        cols = pl.ds(pl.multiple_of(i * CT, CT), CT)
        own[:, cols] = switch * jnp.dot(shared, sd[:, cols], preferred_element_type=F32)

    ag[0].wait_recv()
    ag.append(gather_step(2, block(L1), block(L2), right))
    ag[1].wait_recv()
    ag.append(gather_step(3, block(R1), block(R2), left))
    metas[L1].wait_recv()
    metas[R1].wait_recv()
    out[1] = select(1)

    ag[2].wait_recv()
    ag.append(gather_step(4, block(L2), block(L3), right))
    ag[3].wait_recv()
    ag.append(gather_step(5, block(R2), block(R3), left))
    metas[L2].wait_recv()
    metas[R2].wait_recv()
    out[2] = select(2)

    down_y.wait_recv()
    down_x = []
    for dx in range(1, NX):
        part = wd2.at[c, :, quarter]
        copy = pltpu.make_async_remote_copy(
            part, part, d_send.at[dx], d_recv.at[dx],
            device_id={"dp": lax.rem(x_at + dx, NX), "ep": ep}, device_id_type=MESH,
        )
        copy.start()
        down_x.append(copy)

    for load in loads[3:]:
        load.wait()
    arrived(out[0])
    run_expert(0)

    ag[4].wait_recv()
    ag.append(gather_step(6, block(L3, 0, 64), block(FAR, 0, 64), right))
    ag[5].wait_recv()
    ag.append(gather_step(7, block(R3, 64, 64), block(FAR, 64, 64), left))
    metas[L3].wait_recv()
    metas[R3].wait_recv()
    out[3] = select(3)

    value_own.wait()
    for copy in by_y:
        copy.wait_recv()
    by_z = []
    for d in range(1, NZ):
        part = vw.at[:, z, c, :, quarter]
        by_z.append(
            remote(
                part, part, vz_send.at[d], vz_recv.at[d], device(y, lax.rem(z + d, NZ), c)
            )
        )
        by_z[-1].start()

    ag[6].wait_recv()
    ag[7].wait_recv()
    metas[FAR].wait_recv()
    out[4] = select(4)

    back = {}
    for chunk in (1, 2, 3):
        arrived(out[chunk])
        run_expert(chunk)
    for copy in down_x:
        copy.wait_recv()
    part = wd2.at[c]
    down_core = remote(part, part, d_send.at[4], d_recv.at[4], device(y, z, 1 - c))
    down_core.start()
    for copy in by_z:
        copy.wait_recv()
    by_x = []
    for dx in range(1, NX):
        part = vw.at[:, :, c, :, quarter]
        copy = pltpu.make_async_remote_copy(
            part, part, vx_send.at[dx], vx_recv.at[dx],
            device_id={"dp": lax.rem(x_at + dx, NX), "ep": ep}, device_id_type=MESH,
        )
        copy.start()
        by_x.append(copy)
    arrived(out[4])
    run_expert(4)
    back[4] = give_back(4)
    back[3] = give_back(3)

    rs = {}

    def pass_on(step, h, place, first, rows, target):
        some, cols = pl.ds(place * T + first, rows), pl.ds(h * HALF, HALF)
        copy = remote(
            rs_send.at[some, cols], rs_recv.at[some, cols], rs_s.at[h, step], rs_r.at[h, step], target
        )
        copy.start()
        rs[step, h] = copy

    def tiles(h, body):
        @pl.loop(h * HALF // CT, (h + 1) * HALF // CT)
        def _(i):
            body(pl.ds(pl.multiple_of(i * CT, CT), CT))

    w4 = weights_of(4)
    down_core.wait_recv()
    returned(4)
    back[2] = give_back(2)
    for copy in ag:
        copy.wait_send()

    def far_part(cols):
        part = weigh(4, w4, cols)
        rs_send[pl.ds(FAR * T, T), cols] = part[0:T, :].astype(BF16)
        own[:, cols] += part[T:, :]

    for h in range(2):
        tiles(h, far_part)
        pass_on(0, h, FAR, 0, 64, left)
        pass_on(1, h, FAR, 64, 64, right)

    def add_block(chunk, step):
        w = weights_of(chunk)
        returned(chunk)
        if chunk == 3:
            back[1] = give_back(1)
        if chunk == 2:
            back[0] = give_back(0)
        first = CHUNKS[chunk][2]
        if chunk == 3:
            got_left, got_right = pl.ds(FAR * T, 64), pl.ds(FAR * T + 64, 64)
        else:
            got_left, got_right = pl.ds((first + 2) * T, T), pl.ds((first + 3) * T, T)

        def add(cols):
            part = weigh(chunk, w, cols)
            a = rs_recv[got_left, cols].astype(F32)
            b = rs_recv[got_right, cols].astype(F32)
            if chunk == 3:
                more = jnp.concatenate([a, jnp.zeros((T, CT), F32), b], axis=0)
            else:
                more = jnp.concatenate([a, b], axis=0)
            rs_send[pl.ds(first * T, 2 * T), cols] = (part + more).astype(BF16)

        for h in range(2):
            rs[step - 2, h].wait_recv()
            rs[step - 1, h].wait_recv()
            tiles(h, add)
            pass_on(step, h, first, 0, T, left)
            pass_on(step + 1, h, first + 1, 0, T, right)

    add_block(3, 2)
    add_block(2, 4)

    for copy in by_x:
        copy.wait_recv()
    part = vw.at[:, :, c, :, :]
    by_core = remote(part, part, vx_send.at[0], vx_recv.at[0], device(y, z, 1 - c))
    by_core.start()

    add_block(1, 6)

    w0 = weights_of(0)
    returned(0)

    @pl.loop(0, D // CT)
    def _(i):
        cols = pl.ds(pl.multiple_of(i * CT, CT), CT)
        own[:, cols] += weigh(0, w0, cols)

    for h in range(2):
        rs[6, h].wait_recv()
        rs[7, h].wait_recv()
    mixture = (
        own[...]
        + rs_recv[pl.ds(L1 * T, T), :].astype(F32)
        + rs_recv[pl.ds(R1 * T, T), :].astype(F32)
    )
    mix_out[...] = mixture.astype(BF16)
    after = tokens[...].astype(F32) + mixture
    scale = lax.rsqrt(jnp.mean(after * after, axis=-1, keepdims=True) + 1e-06)
    xs[own_rows, :] = (after * scale * post_gain[...]).astype(BF16)

    by_core.wait_recv()

    def convolve(cols, first, rows):
        total = conv_w[0:1, cols] * wide[first + 13 : first + 13 + rows, cols]
        for j in range(1, 4):
            total = total + conv_w[j : j + 1, cols] * wide[first + 13 + j : first + 13 + j + rows, cols]
        conv_out[first : first + rows, cols] = silu(total).astype(BF16)

    halo = []
    for i in range(D // CT):
        cols = pl.ds(i * CT, CT)
        vals = jnp.dot(
            xs[own_rows, :], vw[:, :, :, :, cols].reshape(D, CT), preferred_element_type=F32
        ).astype(BF16)
        tail[:, cols] = vals[T - 16 :, :]
        halo.append(
            remote(
                tail.at[:, cols], got.at[:, cols], halo_send.at[i], halo_recv.at[i],
                lax.rem(ep + 1, n_ep),
            )
        )
        halo[-1].start()
        wide[16 : 16 + T, cols] = vals.astype(F32)
        convolve(cols, 16, T - 16)
    before = jnp.where(ep > 0, 1.0, 0.0)
    for i in range(D // CT):
        cols = pl.ds(i * CT, CT)
        halo[i].wait_recv()
        wide[0:16, cols] = got[:, cols].astype(F32) * before
        convolve(cols, 0, 16)

    for copy in list(rs.values()) + list(metas.values()) + by_y + by_z + by_x + [by_core] + halo + [down_y] + down_x + [down_core]:
        copy.wait_send()
    for sent in back.values():
        for copy in sent[0]:
            copy.wait_send()


def local(
    tokens,
    routes,
    gate_share,
    norm_gain,
    w_gate,
    w_up,
    w_down,
    shared_gate,
    shared_up,
    shared_down,
    shared_switch,
    post_gain,
    value_w,
    conv_w,
):
    routes_t = routes.T
    share_t = gate_share.T
    vmem = pl.BlockSpec(memory_space=pltpu.VMEM)
    hbm = pl.BlockSpec(memory_space=pl.ANY)
    dma = pltpu.SemaphoreType.DMA
    return pl.pallas_call(
        moe_kernel,
        out_shape=(jax.ShapeDtypeStruct((T, D), BF16), jax.ShapeDtypeStruct((T, D), BF16)),
        in_specs=[vmem] * 7 + [hbm] * 7,
        out_specs=(vmem, vmem),
        scratch_shapes=[
            pltpu.VMEM((8 * T, D), BF16),
            pltpu.VMEM((NZ, 16, T), F32),
            pltpu.VMEM((8, 16, T), F32),
            pltpu.VMEM((SLOT_ROWS, D), BF16),
            pltpu.VMEM((SLOT_ROWS, D), BF16),
            pltpu.VMEM((SLOT_ROWS, D), BF16),
            pltpu.VMEM((SLOT_ROWS, FF), BF16),
            pltpu.VMEM((T, D), F32),
            pltpu.VMEM((8 * T, D), BF16),
            pltpu.VMEM((D, FF), BF16),
            pltpu.VMEM((D, FF), BF16),
            pltpu.VMEM((FF, D), BF16),
            pltpu.VMEM(shared_gate.shape, BF16),
            pltpu.VMEM(shared_up.shape, BF16),
            pltpu.VMEM(shared_down.shape, BF16),
            pltpu.VMEM((NY, NZ, 2, 32, D), BF16),
            pltpu.VMEM((2, FF, D), BF16),
            pltpu.VMEM((2, NP * CAP, FF), BF16),
            pltpu.VMEM((16 + T, D), F32),
            pltpu.VMEM((16, D), BF16),
            pltpu.VMEM((16, D), BF16),
            dma((7,)),
            dma((8,)),
            dma((8,)),
            dma((8,)),
            dma((8,)),
            dma((5, 8)),
            dma((5, 8)),
            dma((5, 8)),
            dma((5, 8)),
            dma((2, 5)),
            dma((2, 8)),
            dma((2, 8)),
            dma((4,)),
            dma((4,)),
            dma((8,)),
            dma((8,)),
            dma((4,)),
            dma((4,)),
            dma((4,)),
            dma((4,)),
            dma((5,)),
            dma((5,)),
        ],
        compiler_params=pltpu.CompilerParams(
            collective_id=0, has_side_effects=True, vmem_limit_bytes=60 * MiB
        ),
        cost_estimate=pl.CostEstimate(
            flops=13 * 10**9, bytes_accessed=500 * 10**6, transcendentals=0
        ),
        name="experts",
    )(
        tokens,
        routes_t,
        share_t,
        norm_gain.reshape(1, D),
        shared_switch.reshape(D // 128, 128),
        post_gain.reshape(1, D),
        conv_w,
        w_gate.reshape(D, FF),
        w_up.reshape(D, FF),
        w_down.reshape(FF, D),
        shared_gate,
        shared_up,
        shared_down,
        value_w,
    )


def solution(mesh):
    placed = (
        P(("dp", "ep"), None),
        P(("dp", "ep"), None),
        P(("dp", "ep"), None),
        P(),
        P("ep", None, None),
        P("ep", None, None),
        P("ep", None, None),
        P(),
        P(),
        P(),
        P(),
        P(),
        P("ep", None),
        P(),
    )
    return jax.shard_map(
        local,
        mesh=mesh,
        in_specs=placed,
        out_specs=(P(("dp", "ep"), None), P(("dp", "ep"), None)),
        check_vma=False,
    )
```

```python
import jax
import jax.numpy as jnp
from jax import lax
from jax.experimental import pallas as pl
from jax.experimental.pallas import tpu as pltpu
from jax.sharding import PartitionSpec as P

MESH = pl.DeviceIdType.MESH
F32, BF16 = jnp.float32, jnp.bfloat16
NX, NY, NZ, NP = 4, 4, 8, 8
CAP = 24
T = 128
D = 2048
FF = 512
CT = 512
HALF = D // 2
MiB = 2**20

FAR, OWN, L1, R1, L2, R2, L3, R3 = range(8)
SRC_DIST = (4, 0, 1, 7, 2, 6, 3, 5)
CHUNKS = (
    (16, 0, OWN, 1),
    (48, 128, L1, 2),
    (48, 512, L2, 2),
    (48, 896, L3, 2),
    (32, 1280, FAR, 2),
)
SLOT_ROWS = NP * 192
ORDER = [(0, 0), (0, 1), (1, 0), (1, 1), (3, 0), (3, 1), (2, 0), (2, 1)]
PEERS = ORDER[1:]
NEAR = 6


def place_of():
    ep = lax.axis_index("ep")
    return ep // (2 * NZ), lax.rem(ep // 2, NZ), lax.rem(ep, 2)


def device(y, z, c):
    return (y * NZ + z) * 2 + c


def remote(src, dst, send, recv, target):
    return pltpu.make_async_remote_copy(
        src, dst, send, recv, device_id={"ep": target}, device_id_type=MESH
    )


def silu(v):
    return v * (1.0 / (1.0 + jnp.exp(-v)))


def chunk_keys(meta, chunk):
    if chunk == 0:
        return meta[OWN, 0:8, :]
    if chunk == 4:
        own = meta[OWN, 0:8, :]
        own = jnp.where(own >= 16.0, own + 8.0, -1000.0)
        return jnp.concatenate([meta[FAR, 0:8, :], own], axis=1)
    first = CHUNKS[chunk][2]
    return jnp.concatenate([meta[first, 0:8, :], meta[first + 1, 0:8, :] + 24.0], axis=1)


def chunk_shares(meta, chunk):
    first, blocks = CHUNKS[chunk][2:]
    if blocks == 1:
        return meta[first, 8:16, :]
    return jnp.concatenate([meta[first, 8:16, :], meta[first + 1, 8:16, :]], axis=1)


def chunk_matches(meta, chunk):
    rows = CHUNKS[chunk][0]
    keys = chunk_keys(meta, chunk)
    number = lax.broadcasted_iota(jnp.int32, (rows, keys.shape[1]), 0).astype(F32)
    return [keys[p : p + 1, :] == number for p in range(NP)]


def moe_kernel(
    tokens,
    routes_t,
    share_t,
    norm_gain,
    switch_w,
    post_gain,
    conv_w,
    w_gate,
    w_up,
    w_down,
    s_gate,
    s_up,
    s_down,
    value_w,
    mix_out,
    conv_out,
    xs,
    meta_src,
    meta,
    g,
    r,
    v,
    hid,
    own,
    rs_recv,
    wg,
    wu,
    wd,
    sg,
    su,
    sd,
    vw,
    wd2,
    far_hid,
    wide,
    tail,
    got,
    w_sem,
    ag_send,
    ag_recv,
    meta_send,
    meta_recv,
    y_send,
    y_recv,
    b_send,
    b_recv,
    loc_sem,
    rs_s,
    rs_r,
    vy_send,
    vy_recv,
    vz_send,
    vz_recv,
    vx_send,
    vx_recv,
    halo_send,
    halo_recv,
    d_send,
    d_recv,
):
    o, rs_send = g, xs
    x_at, ep, n_ep = lax.axis_index("dp"), lax.axis_index("ep"), 2 * NY * NZ
    y, z, c = place_of()
    me = y * 2 + c
    barrier = pltpu.get_barrier_semaphore()
    right = device(y, lax.rem(z + 1, NZ), c)
    left = device(y, lax.rem(z + NZ - 1, NZ), c)

    def peer(dy, dc):
        return lax.rem(y + dy, NY), lax.rem(c + dc, 2)

    for d in range(1, NZ):
        pl.semaphore_signal(
            barrier, 1, device_id={"ep": device(y, lax.rem(z + d, NZ), c)}, device_id_type=MESH
        )
    for dy, dc in PEERS:
        py, pc = peer(dy, dc)
        pl.semaphore_signal(barrier, 1, device_id={"ep": device(py, z, pc)}, device_id_type=MESH)
    for dx in range(1, NX):
        pl.semaphore_signal(
            barrier, 1, device_id={"dp": lax.rem(x_at + dx, NX), "ep": ep}, device_id_type=MESH
        )
    pl.semaphore_signal(
        barrier, 1, device_id={"ep": lax.rem(ep + n_ep - 1, n_ep)}, device_id_type=MESH
    )

    loads = [
        pltpu.make_async_copy(a, b, w_sem.at[i])
        for i, (a, b) in enumerate(
            ((s_gate, sg), (s_up, su), (s_down, sd), (w_gate, wg), (w_up, wu), (w_down, wd))
        )
    ]
    for load in loads:
        load.start()
    quarter = pl.ds(pl.multiple_of(x_at * (D // NX), D // NX), D // NX)
    value_own = pltpu.make_async_copy(
        value_w.at[:, quarter], vw.at[y, z, c, :, quarter], w_sem.at[6]
    )
    value_own.start()

    own_rows = pl.ds(OWN * T, T)
    resid = tokens[...].astype(F32)
    scale = lax.rsqrt(jnp.mean(resid * resid, axis=-1, keepdims=True) + 1e-06)
    xs[own_rows, :] = (resid * scale * norm_gain[...]).astype(BF16)

    pl.semaphore_wait(barrier, NZ - 1 + len(PEERS) + NX - 1 + 1)

    def block(place, first=0, rows=T):
        return xs.at[pl.ds(place * T + first, rows), :]

    def gather_step(i, src, dst, target):
        copy = remote(src, dst, ag_send.at[i], ag_recv.at[i], target)
        copy.start()
        return copy

    ag = [
        gather_step(0, block(OWN), block(L1), right),
        gather_step(1, block(OWN), block(R1), left),
    ]

    row = lax.broadcasted_iota(jnp.int32, (64, T), 0)
    in_col = lax.rem(row, 8)
    expert = (in_col // 2) * (2 * NZ) + (row // 8) * 2 + lax.rem(in_col, 2)
    gate = share_t[...]
    share = gate / jnp.sum(gate, axis=0, keepdims=True)
    named = jnp.zeros((64, T), F32)
    weight = jnp.zeros((64, T), F32)
    for k in range(10):
        hit = routes_t[k : k + 1, :] == expert
        named = named + jnp.where(hit, 1.0, 0.0)
        weight = weight + jnp.where(hit, share[k : k + 1, :], 0.0)
    earlier = lax.broadcasted_iota(jnp.int32, (T, T), 0) < lax.broadcasted_iota(
        jnp.int32, (T, T), 1
    )
    count = jnp.dot(
        named.astype(BF16), jnp.where(earlier, 1.0, 0.0).astype(BF16), preferred_element_type=F32
    )
    slot = jnp.where(named > 0.0, count, -1000.0)
    for col in range(NZ):
        meta_src[col, 0:8, :] = slot[col * 8 : col * 8 + 8, :]
        meta_src[col, 8:16, :] = weight[col * 8 : col * 8 + 8, :]
    meta[OWN] = meta_src[z]
    metas = {}
    for place, d in enumerate(SRC_DIST):
        if d:
            col = lax.rem(z + d, NZ)
            metas[place] = remote(
                meta_src.at[col], meta.at[place], meta_send.at[place], meta_recv.at[place],
                device(y, col, c),
            )
            metas[place].start()

    def peer_rows(chunk, p):
        rows, base = CHUNKS[chunk][:2]
        return pl.ds(pl.multiple_of(base + p * rows, 16), rows)

    def order_rows(chunk, q, n=1):
        rows, base = CHUNKS[chunk][:2]
        return pl.ds(base + q * rows, n * rows)

    def send_out(chunk):
        copies = []
        for q, (dy, dc) in enumerate(ORDER):
            py, pc = peer(dy, dc)
            src = g.at[peer_rows(chunk, py * 2 + pc), :]
            dst = r.at[order_rows(chunk, q), :]
            if q:
                copies.append(
                    remote(src, dst, y_send.at[chunk, q], y_recv.at[chunk, q], device(py, z, pc))
                )
            else:
                here = pltpu.make_async_copy(src, dst, loc_sem.at[0, chunk])
        for copy in copies:
            copy.start()
        here.start()
        return copies, here

    def far_rows(chunk):
        rows, base = CHUNKS[chunk][:2]
        return pl.ds(base // NP, rows)

    def give_back(chunk):
        copies = []
        for q, (dy, dc) in enumerate(ORDER):
            py, pc = peer((NY - dy) % NY, dc)
            if q < NEAR:
                src, dst = o.at[order_rows(chunk, q), :], v.at[peer_rows(chunk, me), :]
            else:
                src, dst = hid.at[order_rows(chunk, q), :], far_hid.at[c, far_rows(chunk), :]
            if q:
                copies.append(
                    remote(src, dst, b_send.at[chunk, q], b_recv.at[chunk, q], device(py, z, pc))
                )
            else:
                here = pltpu.make_async_copy(src, dst, loc_sem.at[1, chunk])
        for copy in copies[::-1]:
            copy.start()
        here.start()
        return copies, here

    def select(chunk):
        rows, base, first, blocks = CHUNKS[chunk]
        pick = jnp.concatenate(
            [jnp.where(m, 1.0, 0.0) for m in chunk_matches(meta, chunk)], axis=0
        ).astype(BF16)

        @pl.loop(0, D // CT)
        def _(i):
            cols = pl.ds(pl.multiple_of(i * CT, CT), CT)
            g[pl.ds(base, NP * rows), cols] = jnp.dot(
                pick, xs[pl.ds(first * T, blocks * T), cols], preferred_element_type=F32
            ).astype(BF16)

        return send_out(chunk)

    def arrived(sent):
        for copy in sent[0]:
            copy.wait_recv()
        sent[1].wait()

    def run_expert(chunk):
        rows, base = CHUNKS[chunk][:2]
        for copy in out[chunk][0]:
            copy.wait_send()
        some = order_rows(chunk, 0, NP)
        near = order_rows(chunk, 0, NEAR)

        @pl.loop(0, FF // 256)
        def _(i):
            cols = pl.ds(pl.multiple_of(i * 256, 256), 256)
            gate_act = jnp.dot(r[some, :], wg[:, cols], preferred_element_type=F32)
            up_act = jnp.dot(r[some, :], wu[:, cols], preferred_element_type=F32)
            hid[some, cols] = (silu(gate_act) * up_act).astype(BF16)

        @pl.loop(0, D // CT)
        def _(i):
            cols = pl.ds(pl.multiple_of(i * CT, CT), CT)
            o[near, cols] = jnp.dot(hid[near, :], wd[:, cols], preferred_element_type=F32).astype(
                BF16
            )

    def returned(chunk):
        copies, here = back[chunk]
        for copy in copies[NEAR - 1 :]:
            copy.wait_recv()
        py = lax.rem(y + 2, NY)

        @pl.loop(0, D // CT)
        def _(i):
            cols = pl.ds(pl.multiple_of(i * CT, CT), CT)
            for e in range(2):
                v[peer_rows(chunk, py * 2 + e), cols] = jnp.dot(
                    far_hid[e, far_rows(chunk), :], wd2[e, :, cols], preferred_element_type=F32
                ).astype(BF16)

        for copy in copies[: NEAR - 1]:
            copy.wait_recv()
        here.wait()

    def weights_of(chunk):
        shares = chunk_shares(meta, chunk)
        w = jnp.concatenate(
            [
                jnp.where(m, shares[p : p + 1, :], 0.0)
                for p, m in enumerate(chunk_matches(meta, chunk))
            ],
            axis=0,
        )
        high = w.astype(BF16)
        return high, (w - high.astype(F32)).astype(BF16)

    def weigh(chunk, w, cols):
        rows, base = CHUNKS[chunk][:2]
        vals = v[pl.ds(base, NP * rows), cols]
        dims = (((0,), (0,)), ((), ()))
        return lax.dot_general(w[0], vals, dims, preferred_element_type=F32) + lax.dot_general(
            w[1], vals, dims, preferred_element_type=F32
        )

    out = {0: select(0)}
    down_y = remote(
        w_down.at[:, quarter], wd2.at[c, :, quarter], d_send.at[0], d_recv.at[0],
        device(lax.rem(y + 2, NY), z, c),
    )
    down_y.start()
    by_y = []
    for dy in range(1, NY):
        by_y.append(
            remote(
                value_w.at[:, quarter], vw.at[y, z, c, :, quarter], vy_send.at[dy], vy_recv.at[dy],
                device(lax.rem(y + dy, NY), z, c),
            )
        )
        by_y[-1].start()

    for load in loads[:3]:
        load.wait()
    n_own = xs[own_rows, :]
    switch_sum = jnp.zeros((T, 128), F32)
    switch_row = switch_w[...].astype(F32)
    for i in range(D // 128):
        part = xs[own_rows, pl.ds(i * 128, 128)].astype(F32)
        switch_sum = switch_sum + part * switch_row[i : i + 1, :]
    switch_sum = jnp.sum(switch_sum, axis=-1, keepdims=True)
    switch = 1.0 / (1.0 + jnp.exp(-switch_sum))
    shared = (
        silu(jnp.dot(n_own, sg[...], preferred_element_type=F32))
        * jnp.dot(n_own, su[...], preferred_element_type=F32)
    ).astype(BF16)

    @pl.loop(0, D // CT)
    def _(i):
        cols = pl.ds(pl.multiple_of(i * CT, CT), CT)
        own[:, cols] = switch * jnp.dot(shared, sd[:, cols], preferred_element_type=F32)

    ag[0].wait_recv()
    ag.append(gather_step(2, block(L1), block(L2), right))
    ag[1].wait_recv()
    ag.append(gather_step(3, block(R1), block(R2), left))
    metas[L1].wait_recv()
    metas[R1].wait_recv()
    out[1] = select(1)

    ag[2].wait_recv()
    ag.append(gather_step(4, block(L2), block(L3), right))
    ag[3].wait_recv()
    ag.append(gather_step(5, block(R2), block(R3), left))
    metas[L2].wait_recv()
    metas[R2].wait_recv()
    out[2] = select(2)

    down_y.wait_recv()
    down_x = []
    for dx in range(1, NX):
        part = wd2.at[c, :, quarter]
        copy = pltpu.make_async_remote_copy(
            part, part, d_send.at[dx], d_recv.at[dx],
            device_id={"dp": lax.rem(x_at + dx, NX), "ep": ep}, device_id_type=MESH,
        )
        copy.start()
        down_x.append(copy)

    for load in loads[3:]:
        load.wait()
    arrived(out[0])
    run_expert(0)

    ag[4].wait_recv()
    ag.append(gather_step(6, block(L3, 0, 64), block(FAR, 0, 64), right))
    ag[5].wait_recv()
    ag.append(gather_step(7, block(R3, 64, 64), block(FAR, 64, 64), left))
    metas[L3].wait_recv()
    metas[R3].wait_recv()

    value_own.wait()
    for copy in by_y:
        copy.wait_recv()
    by_z = []
    for d in range(1, NZ):
        part = vw.at[:, z, c, :, quarter]
        by_z.append(
            remote(
                part, part, vz_send.at[d], vz_recv.at[d], device(y, lax.rem(z + d, NZ), c)
            )
        )
        by_z[-1].start()

    ag[6].wait_recv()
    ag[7].wait_recv()
    metas[FAR].wait_recv()
    out[4] = select(4)
    out[3] = select(3)

    back = {}
    for chunk in (1, 2):
        arrived(out[chunk])
        run_expert(chunk)
    for copy in down_x:
        copy.wait_recv()
    part = wd2.at[c]
    down_core = remote(part, part, d_send.at[4], d_recv.at[4], device(y, z, 1 - c))
    down_core.start()
    for copy in by_z:
        copy.wait_recv()
    by_x = []
    for dx in range(1, NX):
        part = vw.at[:, :, c, :, quarter]
        copy = pltpu.make_async_remote_copy(
            part, part, vx_send.at[dx], vx_recv.at[dx],
            device_id={"dp": lax.rem(x_at + dx, NX), "ep": ep}, device_id_type=MESH,
        )
        copy.start()
        by_x.append(copy)
    arrived(out[4])
    run_expert(4)
    back[4] = give_back(4)
    arrived(out[3])
    run_expert(3)
    back[3] = give_back(3)

    rs = {}

    def pass_on(step, h, place, first, rows, target):
        some, cols = pl.ds(place * T + first, rows), pl.ds(h * HALF, HALF)
        copy = remote(
            rs_send.at[some, cols], rs_recv.at[some, cols], rs_s.at[h, step], rs_r.at[h, step], target
        )
        copy.start()
        rs[step, h] = copy

    def tiles(h, body):
        @pl.loop(h * HALF // CT, (h + 1) * HALF // CT)
        def _(i):
            body(pl.ds(pl.multiple_of(i * CT, CT), CT))

    w4 = weights_of(4)
    down_core.wait_recv()
    returned(4)
    back[2] = give_back(2)
    for copy in ag:
        copy.wait_send()

    def far_part(cols):
        part = weigh(4, w4, cols)
        rs_send[pl.ds(FAR * T, T), cols] = part[0:T, :].astype(BF16)
        own[:, cols] += part[T:, :]

    for h in range(2):
        tiles(h, far_part)
        pass_on(0, h, FAR, 0, 64, left)
        pass_on(1, h, FAR, 64, 64, right)

    def add_block(chunk, step):
        w = weights_of(chunk)
        returned(chunk)
        if chunk == 3:
            back[1] = give_back(1)
        if chunk == 2:
            back[0] = give_back(0)
        first = CHUNKS[chunk][2]
        if chunk == 3:
            got_left, got_right = pl.ds(FAR * T, 64), pl.ds(FAR * T + 64, 64)
        else:
            got_left, got_right = pl.ds((first + 2) * T, T), pl.ds((first + 3) * T, T)

        def add(cols):
            part = weigh(chunk, w, cols)
            a = rs_recv[got_left, cols].astype(F32)
            b = rs_recv[got_right, cols].astype(F32)
            if chunk == 3:
                more = jnp.concatenate([a, jnp.zeros((T, CT), F32), b], axis=0)
            else:
                more = jnp.concatenate([a, b], axis=0)
            rs_send[pl.ds(first * T, 2 * T), cols] = (part + more).astype(BF16)

        for h in range(2):
            rs[step - 2, h].wait_recv()
            rs[step - 1, h].wait_recv()
            tiles(h, add)
            pass_on(step, h, first, 0, T, left)
            pass_on(step + 1, h, first + 1, 0, T, right)

    add_block(3, 2)
    for copy in by_x:
        copy.wait_recv()
    part = vw.at[:, :, c, :, :]
    by_core = remote(part, part, vx_send.at[0], vx_recv.at[0], device(y, z, 1 - c))
    by_core.start()

    add_block(2, 4)

    add_block(1, 6)

    w0 = weights_of(0)
    returned(0)

    @pl.loop(0, D // CT)
    def _(i):
        cols = pl.ds(pl.multiple_of(i * CT, CT), CT)
        own[:, cols] += weigh(0, w0, cols)

    squares = jnp.zeros((T, 1), F32)
    for h in range(2):
        rs[6, h].wait_recv()
        rs[7, h].wait_recv()
        cols = pl.ds(h * HALF, HALF)
        mixture = (
            own[:, cols]
            + rs_recv[pl.ds(L1 * T, T), cols].astype(F32)
            + rs_recv[pl.ds(R1 * T, T), cols].astype(F32)
        )
        mix_out[:, cols] = mixture.astype(BF16)
        after = tokens[:, cols].astype(F32) + mixture
        own[:, cols] = after
        squares = squares + jnp.sum(after * after, axis=-1, keepdims=True)
    scale = lax.rsqrt(squares * (1.0 / D) + 1e-06)
    xs[own_rows, :] = (own[...] * scale * post_gain[...]).astype(BF16)

    by_core.wait_recv()

    def convolve(cols, first, rows):
        total = conv_w[0:1, cols] * wide[first + 13 : first + 13 + rows, cols]
        for j in range(1, 4):
            total = total + conv_w[j : j + 1, cols] * wide[first + 13 + j : first + 13 + j + rows, cols]
        conv_out[first : first + rows, cols] = silu(total).astype(BF16)

    halo = []
    for i in range(D // CT):
        cols = pl.ds(i * CT, CT)
        vals = jnp.dot(
            xs[own_rows, :], vw[:, :, :, :, cols].reshape(D, CT), preferred_element_type=F32
        ).astype(BF16)
        tail[:, cols] = vals[T - 16 :, :]
        halo.append(
            remote(
                tail.at[:, cols], got.at[:, cols], halo_send.at[i], halo_recv.at[i],
                lax.rem(ep + 1, n_ep),
            )
        )
        halo[-1].start()
        wide[16 : 16 + T, cols] = vals.astype(F32)
        convolve(cols, 16, T - 16)
    before = jnp.where(ep > 0, 1.0, 0.0)
    for i in range(D // CT):
        cols = pl.ds(i * CT, CT)
        halo[i].wait_recv()
        wide[0:16, cols] = got[:, cols].astype(F32) * before
        convolve(cols, 0, 16)

    for copy in list(rs.values()) + list(metas.values()) + by_y + by_z + by_x + [by_core] + halo + [down_y] + down_x + [down_core]:
        copy.wait_send()
    for sent in back.values():
        for copy in sent[0]:
            copy.wait_send()


def hand_on(mix, conv, mix_out, conv_out):
    mix_out[...] = mix[...]
    conv_out[...] = conv[...]


def local(
    tokens,
    routes,
    gate_share,
    norm_gain,
    w_gate,
    w_up,
    w_down,
    shared_gate,
    shared_up,
    shared_down,
    shared_switch,
    post_gain,
    value_w,
    conv_w,
):
    routes_t = routes.T
    share_t = gate_share.T
    vmem = pl.BlockSpec(memory_space=pltpu.VMEM)
    hbm = pl.BlockSpec(memory_space=pl.ANY)
    dma = pltpu.SemaphoreType.DMA
    mix, conv = pl.pallas_call(
        moe_kernel,
        out_shape=(jax.ShapeDtypeStruct((T, D), BF16), jax.ShapeDtypeStruct((T, D), BF16)),
        in_specs=[vmem] * 7 + [hbm] * 7,
        out_specs=(vmem, vmem),
        scratch_shapes=[
            pltpu.VMEM((8 * T, D), BF16),
            pltpu.VMEM((NZ, 16, T), F32),
            pltpu.VMEM((8, 16, T), F32),
            pltpu.VMEM((SLOT_ROWS, D), BF16),
            pltpu.VMEM((SLOT_ROWS, D), BF16),
            pltpu.VMEM((SLOT_ROWS, D), BF16),
            pltpu.VMEM((SLOT_ROWS, FF), BF16),
            pltpu.VMEM((T, D), F32),
            pltpu.VMEM((8 * T, D), BF16),
            pltpu.VMEM((D, FF), BF16),
            pltpu.VMEM((D, FF), BF16),
            pltpu.VMEM((FF, D), BF16),
            pltpu.VMEM(shared_gate.shape, BF16),
            pltpu.VMEM(shared_up.shape, BF16),
            pltpu.VMEM(shared_down.shape, BF16),
            pltpu.VMEM((NY, NZ, 2, 32, D), BF16),
            pltpu.VMEM((2, FF, D), BF16),
            pltpu.VMEM((2, NP * CAP, FF), BF16),
            pltpu.VMEM((16 + T, D), F32),
            pltpu.VMEM((16, D), BF16),
            pltpu.VMEM((16, D), BF16),
            dma((7,)),
            dma((8,)),
            dma((8,)),
            dma((8,)),
            dma((8,)),
            dma((5, 8)),
            dma((5, 8)),
            dma((5, 8)),
            dma((5, 8)),
            dma((2, 5)),
            dma((2, 8)),
            dma((2, 8)),
            dma((4,)),
            dma((4,)),
            dma((8,)),
            dma((8,)),
            dma((4,)),
            dma((4,)),
            dma((4,)),
            dma((4,)),
            dma((5,)),
            dma((5,)),
        ],
        compiler_params=pltpu.CompilerParams(
            collective_id=0, has_side_effects=True, vmem_limit_bytes=60 * MiB
        ),
        cost_estimate=pl.CostEstimate(
            flops=13 * 10**9, bytes_accessed=500 * 10**6, transcendentals=0
        ),
        name="experts",
    )(
        tokens,
        routes_t,
        share_t,
        norm_gain.reshape(1, D),
        shared_switch.reshape(D // 128, 128),
        post_gain.reshape(1, D),
        conv_w,
        w_gate.reshape(D, FF),
        w_up.reshape(D, FF),
        w_down.reshape(FF, D),
        shared_gate,
        shared_up,
        shared_down,
        value_w,
    )
    return pl.pallas_call(
        hand_on,
        out_shape=(jax.ShapeDtypeStruct((T, D), BF16), jax.ShapeDtypeStruct((T, D), BF16)),
        in_specs=[vmem, vmem],
        out_specs=(vmem, vmem),
        name="outputs",
    )(mix, conv)


def solution(mesh):
    placed = (
        P(("dp", "ep"), None),
        P(("dp", "ep"), None),
        P(("dp", "ep"), None),
        P(),
        P("ep", None, None),
        P("ep", None, None),
        P("ep", None, None),
        P(),
        P(),
        P(),
        P(),
        P(),
        P("ep", None),
        P(),
    )
    return jax.shard_map(
        local,
        mesh=mesh,
        in_specs=placed,
        out_specs=(P(("dp", "ep"), None), P(("dp", "ep"), None)),
        check_vma=False,
    )
```
